32 devices in a mesh: groups: 2 (over y), elem: 4 (over z), lag: 2 (over x), gust: 2 (over core).
Axes of the slice: x: 2, y: 2, z: 4, core: 2. Of those that a mesh axis runs over, the one named last changes fastest.
Arguments:
- history: float32 [16, 16, 512], P('lag', ('groups', 'gust'), 'elem'), parts along dimension 1, may hold values from -6 to 6
- forcing: float32 [5, 16, 512], P(None, ('groups', 'gust'), 'elem'), parts along dimension 1, may hold values from -6 to 6
- interaction: bfloat16 [16, 512, 512], P('lag', 'elem'), may hold values from -0.09375 to 0.09375
- block_mask: int32 [16, 4, 4], P('lag', 'elem'), may hold values from 0 to 1, as said below
- correction: float32 [512, 128], P('elem'), may hold values from -0.5 to 0.5
- neighbours: int32 [4, 512], P(None, 'elem'), may hold values from 0 to 511, as said below
- edge_coef: float32 [4, 512], P(None, 'elem'), may hold values from -2 to 2
Outputs:
- sources: float32 [5, 16, 512], P(None, ('groups', 'gust'), 'elem'), parts along dimension 1
The draws below stay inside these ranges and needn't reach their ends.
There are 2 independent parts, one for each index of `groups`. The reference program is written for one: setup_inputs(seed, part) draws one part's arguments, and reference() takes and returns one part's arrays. A program takes and returns all parts, laid end to end along the dimension named above; an argument that names none is the same for every part. Nothing has to cross between parts.
Inputs may be any that keep to these rules, and one draw needn't show every extreme that they name: block_mask[l, i, j] is 1 where the elements of block i (the 128 elements of one index of elem) feel block j at lag l + 1, else 0. neighbours[k, e] - e, taken cyclically modulo 512, lies within -8 to 8, and both ends are taken.
All inputs are finite; a program needn't handle non-finite values.
Results may differ from the reference program's by a relative error of at most 0.002.
Values may be sent and summed in bfloat16 or wider, within the bound.
No kernel may reach another device: no remote copies, remote signals or barrier semaphores. Data moves between devices by JAX's collectives and lax.ppermute only.
A program may use at most 64 MiB of HBM per device.

```python
import jax
import jax.numpy as jnp
from jax import lax

ROWS = 128
LAGS = 16
GUSTS = 8
NBRS = 4
RIM = 8
STEPS = 5
ELEMS = 512
BLOCKS = 4


def draw_block_mask(key, part):
    level_key = jax.random.fold_in(key, 11)
    raw_key = jax.random.fold_in(key, 12)
    level = jax.random.randint(level_key, (1, BLOCKS, 1), 1, 9)
    raw = jax.random.randint(raw_key, (LAGS, BLOCKS, BLOCKS), 0, 8)
    return (raw < level).astype(jnp.int32)


def draw_neighbours(key, part):
    offset_key = jax.random.fold_in(key, 21)
    offsets = jax.random.randint(offset_key, (NBRS, ELEMS), -RIM, RIM + 1)
    offsets = offsets.at[0, 0].set(RIM)
    offsets = offsets.at[1, 0].set(-RIM)
    places = jnp.arange(ELEMS, dtype=jnp.int32)
    return ((places[None, :] + offsets) % ELEMS).astype(jnp.int32)


def shard_levels(stream_key, shape, split, smallest, top_value):
    factor_of, own = 1.0, jax.random.fold_in(stream_key, 6)
    for dim, parts in split:
        steps = jnp.exp(jax.random.uniform(jax.random.fold_in(own, dim), (parts,), jnp.float32, smallest / len(split), top_value / len(split)))
        factor_of = factor_of * jnp.repeat(steps, shape[dim] // parts).reshape([-1 if axis == dim else 1 for axis in range(len(shape))])
    return factor_of


def normal_values(key, extent, scale, limit, split=(), kind=jnp.bfloat16):
    result = jax.random.normal(key, extent, jnp.float32) * scale
    if len(split) > 0:
        result = shard_levels(key, extent, split, -0.22, 0.18) * result
    return jnp.clip(result, min=-limit, max=limit).astype(kind)


def setup_inputs(seed: int = 0, part: int = 0) -> dict:
    streams_of = jax.random.split(jax.random.key(seed), 8)
    own_keys = jax.random.split(jax.random.fold_in(streams_of[7], part), 8)
    history = normal_values(own_keys[0], (LAGS, GUSTS, ELEMS), 1.0, 6.0, ((0, 2), (1, 2), (2, 4)), jnp.float32)
    forcing = normal_values(own_keys[1], (STEPS, GUSTS, ELEMS), 1.0, 6.0, ((1, 2), (2, 4)), jnp.float32)
    interaction = normal_values(streams_of[2], (LAGS, ELEMS, ELEMS), (LAGS * ELEMS // 2) ** -0.5, 0.09375, ((0, 2), (1, 4)))
    block_mask = draw_block_mask(jax.random.fold_in(streams_of[7], 71), part)
    correction = normal_values(streams_of[4], (ELEMS, ROWS), ROWS ** -0.5, 0.5, ((0, 4),), jnp.float32)
    neighbours = draw_neighbours(jax.random.fold_in(streams_of[7], 71), part)
    edge_coef = normal_values(streams_of[6], (NBRS, ELEMS), 0.3, 2.0, ((1, 4),), jnp.float32)
    return {"history": history, "forcing": forcing, "interaction": interaction, "block_mask": block_mask, "correction": correction, "neighbours": neighbours, "edge_coef": edge_coef}


def reference(history, forcing, interaction, block_mask, correction, neighbours, edge_coef):
    precise = lax.Precision.HIGHEST
    block_count = block_mask.shape[1]
    row_count = ELEMS // block_count

    def lag_step(carry, inputs):
        hist_lag, coupling, mask_lag = inputs
        spread = jnp.repeat(jnp.repeat(mask_lag.astype(jnp.bfloat16), row_count, 0), row_count, 1)
        live = coupling * spread
        product = jnp.dot(hist_lag.astype(jnp.bfloat16), live.T, preferred_element_type=jnp.float32)
        return carry + product, None

    hist = history
    results = []
    for step in range(STEPS):
        retarded, unused = lax.scan(lag_step, jnp.zeros((GUSTS, ELEMS), jnp.float32), (hist, interaction, block_mask))
        newest = hist[0]
        across = newest[:, neighbours]
        gradient = jnp.sum(edge_coef[None, :, :] * (across - newest[:, None, :]), axis=1)
        drive = forcing[step] - retarded + gradient
        blocked = drive.reshape(GUSTS, block_count, row_count)
        corr_blocks = correction.reshape(block_count, row_count, row_count)
        fresh = blocked + jnp.einsum("gbr,ber->gbe", blocked, corr_blocks, precision=precise)
        fresh = fresh.reshape(GUSTS, ELEMS)
        results.append(fresh)
        hist = jnp.concatenate([fresh[None], hist[:-1]], 0)
    return jnp.stack(results, 0)
```

```python
import jax
import jax.numpy as jnp
from jax import lax
from jax.sharding import PartitionSpec as P

RIM = 8
STEPS = 5
FEW = 4


def gathered(value, dim):
    count = lax.axis_size("elem")
    if count > FEW or count & (count - 1):
        return lax.all_gather(value, "elem", axis=dim, tiled=True)
    place = lax.axis_index("elem")
    pieces = [value] + [
        lax.ppermute(value, "elem", [(i, i ^ flip) for i in range(count)])
        for flip in range(1, count)
    ]
    ordered = []
    for block in range(count):
        chosen = pieces[0]
        for flip in range(1, count):
            chosen = jnp.where(place ^ flip == block, pieces[flip], chosen)
        ordered.append(chosen)
    return jnp.concatenate(ordered, axis=dim)


def on_device(history, forcing, interaction, block_mask, correction, neighbours, edge_coef):
    precise = lax.Precision.HIGHEST
    rows = correction.shape[0]
    blocks = lax.axis_size("elem")
    total = rows * blocks
    lags, gusts, _ = history.shape
    lag_count = lax.axis_size("lag")
    lag_place = lax.axis_index("lag")
    own_start = lax.axis_index("elem") * rows
    late = STEPS - 1
    assert lags >= late

    live = jnp.repeat(block_mask[:, 0, :].astype(jnp.bfloat16), rows, axis=1)
    masked = interaction * live[:, None, :]

    own_places = own_start + jnp.arange(rows, dtype=jnp.int32)
    offsets = (neighbours - own_places[None, :] + RIM) % total
    spread = [
        jnp.sum(jnp.where(offsets == d, edge_coef, 0.0), axis=0) for d in range(2 * RIM + 1)
    ]

    def gradient_of(full):
        wide = jnp.concatenate([full[:, total - RIM :], full, full[:, :RIM]], axis=1)
        window = lax.dynamic_slice(wide, (0, own_start), (gusts, rows + 2 * RIM))
        own = window[:, RIM : RIM + rows]
        out = jnp.zeros_like(own)
        for d in range(2 * RIM + 1):
            if d != RIM:
                out += spread[d][None] * (window[:, d : d + rows] - own)
        return out

    hist = gathered(history.astype(jnp.bfloat16), 2)
    newest = gathered(history[0], 1)
    before = lax.ppermute(
        hist[lags - late :], "lag", [(i, (i + 1) % lag_count) for i in range(lag_count)]
    )
    before = jnp.where(lag_place == 0, jnp.zeros_like(before), before)
    longer = jnp.concatenate([before, hist], axis=0)
    stacked = jnp.stack(
        [longer[late - step : late - step + lags] for step in range(STEPS)], axis=1
    ).reshape(lags, STEPS * gusts, total)
    partial = jnp.einsum("lmc,lrc->mr", stacked, masked, preferred_element_type=jnp.float32)
    known = lax.psum(partial.reshape(STEPS, gusts, rows), "lag")
    base = forcing - known

    fresh_b = []
    results = []
    for step in range(STEPS):
        drive = base[step] + gradient_of(newest)
        if step:
            past = jnp.stack(fresh_b[::-1], axis=0)
            drive -= jnp.einsum(
                "lgc,lrc->gr", past, masked[:step], preferred_element_type=jnp.float32
            )
        fresh = drive + jnp.dot(drive, correction.T, precision=precise)
        results.append(fresh)
        if step < late:
            newest = gathered(fresh, 1)
            fresh_b.append(newest.astype(jnp.bfloat16))
    mine = jnp.stack(results, 0)
    return lax.psum(jnp.where(lag_place == 0, mine, 0.0), "lag")


def solution(mesh):
    placed = (
        P("lag", ("groups", "gust"), "elem"),
        P(None, ("groups", "gust"), "elem"),
        P("lag", "elem", None),
        P("lag", "elem", None),
        P("elem", None),
        P(None, "elem"),
        P(None, "elem"),
    )
    return jax.shard_map(
        on_device,
        mesh=mesh,
        in_specs=placed,
        out_specs=P(None, ("groups", "gust"), "elem"),
        check_vma=False,
    )
```

```python
import jax
import jax.numpy as jnp
from jax import lax
from jax.experimental import pallas as pl
from jax.experimental.pallas import tpu as pltpu
from jax.sharding import PartitionSpec as P

RIM = 8
STEPS = 5
LATE = STEPS - 1
WORDS = 3


def in_words(value):
    out = []
    for _ in range(WORDS):
        head = lax.reduce_precision(value, 8, 7)
        out.append(head.astype(jnp.bfloat16))
        value = value - head
    return out


def from_words(words):
    return words[0].astype(jnp.float32) + (
        words[1].astype(jnp.float32) + words[2].astype(jnp.float32)
    )


def flips(value, flipped=(1, 2, 3)):
    count = lax.axis_size("elem")
    return [value] + [
        lax.ppermute(value, "elem", [(i, i ^ flip) for i in range(count)]) for flip in flipped
    ]


def in_order(pieces, dim):
    place = lax.axis_index("elem")
    ordered = []
    for block in range(len(pieces)):
        chosen = pieces[0]
        for flip in range(1, len(pieces)):
            chosen = jnp.where(place ^ flip == block, pieces[flip], chosen)
        ordered.append(chosen)
    return jnp.concatenate(ordered, axis=dim)


def lag_behind(value):
    count = lax.axis_size("lag")
    moved = lax.ppermute(value, "lag", [(i, (i + 1) % count) for i in range(count)])
    return jnp.where(lax.axis_index("lag") == 0, jnp.zeros_like(moved), moved)


def by_offset(neighbours, edge_coef):
    rows = neighbours.shape[1]
    total = rows * lax.axis_size("elem")
    places = lax.axis_index("elem") * rows + jnp.arange(rows, dtype=jnp.int32)
    return (neighbours - places[None, :] + RIM) % total


def spread_weights(offsets, edge_coef):
    return [
        jnp.sum(jnp.where(offsets == d, edge_coef, 0.0), axis=0, keepdims=True)
        for d in range(2 * RIM + 1)
    ]


def own_gradient(newest, spread):
    rows = spread[0].shape[1]
    total = newest.shape[1]
    wide = jnp.concatenate([newest[:, total - RIM :], newest, newest[:, :RIM]], axis=1)
    start = lax.axis_index("elem") * rows
    window = lax.dynamic_slice(wide, (0, start), (newest.shape[0], rows + 2 * RIM))
    own = window[:, RIM : RIM + rows]
    out = jnp.zeros_like(own)
    for d in range(2 * RIM + 1):
        if d != RIM:
            out += spread[d] * (window[:, d : d + rows] - own)
    return out


def known_part(hist, masked):
    lags, gusts, total = hist.shape
    longer = jnp.concatenate([lag_behind(hist[lags - LATE :]), hist], axis=0)
    stacked = jnp.stack(
        [longer[LATE - step : LATE - step + lags] for step in range(STEPS)], axis=1
    ).reshape(lags, STEPS * gusts, total)
    part = jnp.einsum("lmc,lrc->mr", stacked, masked, preferred_element_type=jnp.float32)
    return part.reshape(STEPS, gusts, masked.shape[1])


def live_coefficients(interaction, block_mask, rows):
    live = jnp.repeat(block_mask[:, 0, :].astype(jnp.bfloat16), rows, axis=1)
    return interaction * live[:, None, :]


def exchange_each_step(
    history, forcing, interaction, block_mask, correction, neighbours, edge_coef
):
    rows = correction.shape[0]
    masked = live_coefficients(interaction, block_mask, rows)
    spread = spread_weights(by_offset(neighbours, edge_coef), edge_coef)

    def gathered(value, dim):
        return lax.all_gather(value, "elem", axis=dim, tiled=True)

    hist = gathered(history.astype(jnp.bfloat16), 2)
    newest = gathered(history[0], 1)
    base = forcing - lax.psum(known_part(hist, masked), "lag")
    fresh_b = []
    results = []
    for step in range(STEPS):
        drive = base[step] + own_gradient(newest, spread)
        if step:
            past = jnp.stack(fresh_b[::-1], axis=0)
            drive -= jnp.einsum(
                "lgc,lrc->gr", past, masked[:step], preferred_element_type=jnp.float32
            )
        fresh = drive + jnp.dot(drive, correction.T, precision=lax.Precision.HIGHEST)
        results.append(fresh)
        if step < LATE:
            newest = gathered(fresh, 1)
            fresh_b.append(newest.astype(jnp.bfloat16))
    first = lax.axis_index("lag") == 0
    return lax.psum(jnp.where(first, jnp.stack(results, 0), 0.0), "lag")


def march(
    own_w, near_w, mid_w, far_w, near_s, mid_s, far_s, own_c,
    base_0, base_1, base_2, base_3, spread_ref,
    own_out, other_out,
    w, c, base, sems,
):
    place = lax.axis_index("elem")
    half = lax.axis_index("gust")
    rows = own_w.shape[1]
    cut = rows // 2
    gusts = base_0.shape[1]
    total = w.shape[2]
    copies = []

    def fetch(source, target):
        copy = pltpu.make_async_copy(source, target, sems.at[len(copies)])
        copy.start()
        copies.append(copy)

    def bring(received, flip, side, lags):
        start = pl.multiple_of((place ^ flip) * rows + side * cut, cut)
        fetch(received.at[pl.ds(0, lags)], w.at[pl.ds(0, lags), pl.ds(start, cut)])
        fetch(received.at[lags], c.at[pl.ds(start, cut)])

    own_start = pl.multiple_of(place * rows, rows)
    fetch(own_w, w.at[:, pl.ds(own_start, rows)])
    fetch(own_c, c.at[pl.ds(own_start, rows)])
    for side, received in ((half, (near_w, mid_w, far_w)), (1 - half, (near_s, mid_s, far_s))):
        bring(received[0], 1, side, LATE)
        bring(received[1], 3, side, LATE - 1)
        bring(received[2], 2, side, LATE - 1)
    for flip, received in enumerate((base_0, base_1, base_2, base_3)):
        start = pl.multiple_of((place ^ flip) * rows, rows)
        base[:, :, pl.ds(start, rows)] = received[...]
    for copy in copies:
        copy.wait()

    pair_start = pl.multiple_of((place // 2) * (2 * rows), 2 * rows)

    def times(fresh_b, lag, start, count):
        return lax.dot_general(
            fresh_b, w[lag, pl.ds(start, count), :], (((1,), (1,)), ((), ())),
            preferred_element_type=jnp.float32,
        )

    def small(lhs, rhs):
        return lax.dot_general(
            lhs, rhs, (((1,), (1,)), ((), ())), preferred_element_type=jnp.float32
        )

    def corrected(drive, starts):
        out = []
        for at, start in enumerate(starts):
            part = drive[:, at * rows : (at + 1) * rows]
            d_hi = part.astype(jnp.bfloat16)
            rest = part - d_hi.astype(jnp.float32)
            d_mid = rest.astype(jnp.bfloat16)
            d_lo = (rest - d_mid.astype(jnp.float32)).astype(jnp.bfloat16)
            c_hi, c_mid, c_lo = (
                c[pl.ds(start, rows), word * rows : (word + 1) * rows] for word in range(WORDS)
            )
            added = small(d_hi, c_lo) + small(d_lo, c_hi) + small(d_mid, c_mid)
            added = added + (small(d_hi, c_mid) + small(d_mid, c_hi))
            out.append(part + (added + small(d_hi, c_hi)))
        return jnp.concatenate(out, axis=1)

    def gradient(newest):
        out = jnp.zeros_like(newest)
        for d in range(2 * RIM + 1):
            if d != RIM:
                moved = pltpu.roll(newest, (RIM - d) % total, 1)
                out += spread_ref[d : d + 1, :] * (moved - newest)
        return out

    def pair_of(value):
        return jnp.where(place < 2, value[:, : 2 * rows], value[:, 2 * rows :])

    def put(step, pair):
        left, right = pair[:, :rows], pair[:, rows:]
        odd = place % 2 == 1
        own_out[step] = jnp.where(odd, right, left)
        other_out[step] = jnp.where(odd, left, right)

    all_blocks = [block * rows for block in range(total // rows)]
    waiting = {step: base[step] for step in range(LATE)}
    waiting[LATE] = pair_of(base[LATE])
    for step in range(LATE):
        fresh = corrected(waiting[step], all_blocks)
        put(step, pair_of(fresh))
        fresh_b = fresh.astype(jnp.bfloat16)
        slope = gradient(fresh)
        for later in range(step + 1, STEPS):
            lag = later - step - 1
            if later < LATE:
                change = times(fresh_b, lag, 0, total)
                if lag == 0:
                    change = change - slope
            else:
                change = times(fresh_b, lag, pair_start, 2 * rows)
                if lag == 0:
                    change = change - pair_of(slope)
            waiting[later] = waiting[later] - change
    put(LATE, corrected(waiting[LATE], [pair_start, pair_start + rows]))


def middle_marches(history, forcing, interaction, block_mask, correction, neighbours, edge_coef):
    rows = correction.shape[0]
    lags, gusts, _ = history.shape
    count = lax.axis_size("elem")
    total = rows * count
    place = lax.axis_index("elem")
    lag_place = lax.axis_index("lag")
    half = lax.axis_index("gust")
    cut = rows // 2

    offsets = by_offset(neighbours, edge_coef).astype(jnp.bfloat16)
    newest_words = in_words(history[0])[1:]
    message = jnp.concatenate(
        [history.astype(jnp.bfloat16)]
        + [word[None] for word in newest_words + [offsets] + in_words(edge_coef)],
        axis=0,
    )
    everyone = in_order(flips(message), 2)
    hist = everyone[:lags]
    newest = from_words([everyone[0], everyone[lags], everyone[lags + 1]])
    all_offsets = everyone[lags + 2].astype(jnp.int32)
    all_coef = from_words([everyone[lags + 3 + word] for word in range(WORDS)])
    spread = spread_weights(all_offsets, all_coef)

    masked = live_coefficients(interaction, block_mask, rows)
    words_c = in_words(correction)
    own_c = jnp.concatenate(words_c + [jnp.zeros_like(words_c[0])], axis=1)
    half_w = lax.dynamic_slice(masked, (0, half * cut, 0), (LATE, cut, total))
    half_c = lax.dynamic_slice(own_c, (half * cut, 0), (cut, total))[None]
    long_load = jnp.concatenate([half_w, half_c], axis=0)
    short_load = jnp.concatenate([half_w[: LATE - 1], half_c], axis=0)

    def at(elem, lag):
        return elem * 2 + lag

    def bulk(load, pairs):
        return lax.ppermute(load, ("elem", "lag"), [(at(a, 0), at(b, 0)) for a, b in pairs])

    near = bulk(long_load, [(0, 1), (3, 2)])
    mid = bulk(short_load, [(1, 2), (2, 1)])
    far = bulk(short_load, [(0, 2), (3, 1)])
    swapped = [lax.ppermute(load, "gust", [(0, 1), (1, 0)]) for load in (near, mid, far)]

    part = known_part(hist, masked)
    known = part + lax.ppermute(part, "lag", [(0, 1), (1, 0)])
    own_spread = [
        lax.dynamic_slice(row, (0, place * rows), (1, rows)) for row in spread
    ]
    slope = own_gradient(newest, own_spread)
    base = jnp.concatenate([(forcing[0] - known[0] + slope)[None], forcing[1:] - known[1:]], 0)
    bases = flips(base)

    vmem = pl.BlockSpec(memory_space=pltpu.VMEM)
    anywhere = pl.BlockSpec(memory_space=pl.ANY)
    shape = jax.ShapeDtypeStruct((STEPS, gusts, rows), jnp.float32)
    own, other = pl.pallas_call(
        march,
        out_shape=(shape, shape),
        in_specs=[anywhere] * 8 + [vmem] * 5,
        out_specs=(vmem, vmem),
        scratch_shapes=[
            pltpu.VMEM((LATE, total, total), jnp.bfloat16),
            pltpu.VMEM((total, total), jnp.bfloat16),
            pltpu.VMEM((STEPS, gusts, total), jnp.float32),
            pltpu.SemaphoreType.DMA((14,)),
        ],
        name="march",
    )(masked[:LATE], near, mid, far, *swapped, own_c, *bases, jnp.concatenate(spread, axis=0))

    def swap(value, flip):
        return lax.ppermute(
            value, ("elem", "lag"), [(i, i ^ flip) for i in range(2 * count)]
        )

    to_lag, to_outer, to_both = swap(own, 1), swap(other, 2), swap(other, 3)
    middle = (place == 1) | (place == 2)
    first = lag_place == 0
    return jnp.where(
        middle, jnp.where(first, own, to_lag), jnp.where(first, to_outer, to_both)
    )


def solution(mesh):
    placed = (
        P("lag", ("groups", "gust"), "elem"),
        P(None, ("groups", "gust"), "elem"),
        P("lag", "elem", None),
        P("lag", "elem", None),
        P("elem", None),
        P(None, "elem"),
        P(None, "elem"),
    )
    small = mesh.shape["elem"] == 4 and mesh.shape["lag"] == 2 and mesh.shape["gust"] == 2
    return jax.shard_map(
        middle_marches if small else exchange_each_step,
        mesh=mesh,
        in_specs=placed,
        out_specs=P(None, ("groups", "gust"), "elem"),
        check_vma=False,
    )
```

```python
import jax
import jax.numpy as jnp
from jax import lax
from jax.experimental import pallas as pl
from jax.experimental.pallas import tpu as pltpu
from jax.sharding import PartitionSpec as P

RIM = 8
STEPS = 5
LATE = STEPS - 1
GUST_ROWS = 8


def flips(value, flipped=(1, 2, 3)):
    count = lax.axis_size("elem")
    return [value] + [
        lax.ppermute(value, "elem", [(i, i ^ flip) for i in range(count)]) for flip in flipped
    ]


def lag_behind(value):
    count = lax.axis_size("lag")
    moved = lax.ppermute(value, "lag", [(i, (i + 1) % count) for i in range(count)])
    return jnp.where(lax.axis_index("lag") == 0, jnp.zeros_like(moved), moved)


def by_offset(neighbours, edge_coef):
    rows = neighbours.shape[1]
    total = rows * lax.axis_size("elem")
    places = lax.axis_index("elem") * rows + jnp.arange(rows, dtype=jnp.int32)
    return (neighbours - places[None, :] + RIM) % total


def spread_weights(offsets, edge_coef):
    return [
        jnp.sum(jnp.where(offsets == d, edge_coef, 0.0), axis=0, keepdims=True)
        for d in range(2 * RIM + 1)
    ]


def own_gradient(newest, spread):
    rows = spread[0].shape[1]
    total = newest.shape[1]
    wide = jnp.concatenate([newest[:, total - RIM :], newest, newest[:, :RIM]], axis=1)
    start = lax.axis_index("elem") * rows
    window = lax.dynamic_slice(wide, (0, start), (newest.shape[0], rows + 2 * RIM))
    own = window[:, RIM : RIM + rows]
    out = jnp.zeros_like(own)
    for d in range(2 * RIM + 1):
        if d != RIM:
            out += spread[d] * (window[:, d : d + rows] - own)
    return out


def known_part(hist, masked):
    lags, gusts, total = hist.shape
    longer = jnp.concatenate([lag_behind(hist[lags - LATE :]), hist], axis=0)
    stacked = jnp.stack(
        [longer[LATE - step : LATE - step + lags] for step in range(STEPS)], axis=1
    ).reshape(lags, STEPS * gusts, total)
    part = jnp.einsum("lmc,lrc->mr", stacked, masked, preferred_element_type=jnp.float32)
    return part.reshape(STEPS, gusts, masked.shape[1])


def live_coefficients(interaction, block_mask, rows):
    live = jnp.repeat(block_mask[:, 0, :].astype(jnp.bfloat16), rows, axis=1)
    return interaction * live[:, None, :]


def exchange_each_step(
    history, forcing, interaction, block_mask, correction, neighbours, edge_coef
):
    rows = correction.shape[0]
    masked = live_coefficients(interaction, block_mask, rows)
    spread = spread_weights(by_offset(neighbours, edge_coef), edge_coef)

    def gathered(value, dim):
        return lax.all_gather(value, "elem", axis=dim, tiled=True)

    hist = gathered(history.astype(jnp.bfloat16), 2)
    newest = gathered(history[0], 1)
    base = forcing - lax.psum(known_part(hist, masked), "lag")
    fresh_b = []
    results = []
    for step in range(STEPS):
        drive = base[step] + own_gradient(newest, spread)
        if step:
            past = jnp.stack(fresh_b[::-1], axis=0)
            drive -= jnp.einsum(
                "lgc,lrc->gr", past, masked[:step], preferred_element_type=jnp.float32
            )
        fresh = drive + jnp.dot(drive, correction.T, precision=lax.Precision.HIGHEST)
        results.append(fresh)
        if step < LATE:
            newest = gathered(fresh, 1)
            fresh_b.append(newest.astype(jnp.bfloat16))
    first = lax.axis_index("lag") == 0
    return lax.psum(jnp.where(first, jnp.stack(results, 0), 0.0), "lag")


def dot_rows(lhs, rhs):
    return lax.dot_general(lhs, rhs, (((1,), (1,)), ((), ())), preferred_element_type=jnp.float32)


def words_of(value, count):
    out = []
    for _ in range(count):
        word = value.astype(jnp.bfloat16)
        out.append(word)
        value = value - word.astype(jnp.float32)
    return out


def pack(history, neighbours, edge_coef, message):
    lags, gusts, rows = history.shape
    total = rows * lax.axis_size("elem")
    places = lax.axis_index("elem") * rows + lax.broadcasted_iota(
        jnp.int32, neighbours.shape, 1
    )
    offsets = lax.rem(neighbours[...] - places + (RIM + total), total)
    pieces = [history[lag] for lag in range(lags)]
    _, mid, low = words_of(history[0], 3)
    pieces += [mid.astype(jnp.float32), low.astype(jnp.float32), offsets.astype(jnp.float32)]
    pieces += [word.astype(jnp.float32) for word in words_of(edge_coef[...], 3)]
    pieces += [jnp.zeros_like(pieces[0])] * (message.shape[0] // gusts - len(pieces))
    message[...] = jnp.concatenate(pieces, axis=0).astype(jnp.bfloat16)


def make_load(mask, interaction, correction, masked, own_c, load):
    lags, rows, total = interaction.shape
    blocks = total // rows
    cut = rows // 2
    for lag in range(lags):
        for block in range(blocks):
            columns = pl.ds(block * rows, rows)
            piece = interaction[lag, :, columns]
            live = mask[lag, block] != 0
            masked[lag, :, columns] = jnp.where(live, piece, jnp.zeros_like(piece))
    own_c[...] = jnp.concatenate(words_of(correction[...], 2), axis=1)
    start = pl.multiple_of(lax.axis_index("gust") * cut, cut)
    for lag in range(LATE - 1):
        load[:, pl.ds(lag * total, total)] = masked[lag, pl.ds(start, cut), :]
    load[:, pl.ds((LATE - 1) * total, 2 * rows)] = own_c[pl.ds(start, cut), :]


def order(piece_0, piece_1, piece_2, piece_3, everyone, late):
    place = lax.axis_index("elem")
    rows = piece_0.shape[1]
    for flip, piece in enumerate((piece_0, piece_1, piece_2, piece_3)):
        start = pl.multiple_of((place ^ flip) * rows, rows)
        everyone[:, pl.ds(start, rows)] = piece[...]
    late[...] = everyone[late.shape[0] : 2 * late.shape[0], :]


def slope_of(newest, spread_ref):
    total = newest.shape[1]
    out = jnp.zeros_like(newest)
    for d in range(2 * RIM):
        shift = d - RIM if d < RIM else d - RIM + 1
        moved = pltpu.roll(newest, (-shift) % total, 1)
        out += spread_ref[d : d + 1, :] * (moved - newest)
    return out


def main_part(everyone, masked, part, slope, spread, longer, slopes):
    lags, rows, total = masked.shape
    gusts = 4
    known = lags * gusts
    wide = everyone[...].astype(jnp.float32)
    longer[...] = jnp.zeros_like(longer)
    longer[LATE * gusts : LATE * gusts + known, :] = wide[:known]
    acc = jnp.zeros(part.shape, jnp.float32)
    for lag in range(lags):
        lhs = longer[lag * gusts : lag * gusts + part.shape[0], :].astype(jnp.bfloat16)
        acc += dot_rows(lhs, masked[lag])
    part[...] = acc

    def piece(index):
        return wide[known + index * gusts : known + (index + 1) * gusts]

    newest = wide[:gusts] + (piece(0) + piece(1))
    offsets = piece(2)
    coef = piece(3) + (piece(4) + piece(5))
    for d in range(2 * RIM):
        value = d if d < RIM else d + 1
        spread[d : d + 1, :] = jnp.sum(
            jnp.where(offsets == float(value), coef, 0.0), axis=0, keepdims=True
        )
    newest = jnp.concatenate([newest, jnp.zeros_like(newest)], axis=0)
    slopes[...] = slope_of(newest, spread)
    start = pl.multiple_of(lax.axis_index("elem") * rows, rows)
    slope[...] = slopes[:, pl.ds(start, rows)]


def late_part(late, masked, part, both, longer):
    gusts = late.shape[0] // LATE
    value = late[...].astype(jnp.float32)
    longer[...] = jnp.zeros_like(longer)
    longer[: late.shape[0], :] = jnp.where(lax.axis_index("lag") == 0, 0.0, value)
    acc = part[...]
    for lag in range(LATE):
        lhs = longer[lag * gusts : lag * gusts + part.shape[0], :].astype(jnp.bfloat16)
        acc += dot_rows(lhs, masked[lag])
    both[...] = acc


def make_base(part, other, forcing, slope, base):
    gusts = forcing.shape[1]
    known = part[...] + other[...]
    for step in range(STEPS):
        at = (STEPS - 1 - step) * gusts
        value = forcing[step] - known[at : at + gusts]
        if step == 0:
            value = value + slope[:gusts]
        base[step] = jnp.concatenate([value, jnp.zeros_like(value)], axis=0)


def march(
    masked, load_1, load_2, load_3, swap_1, swap_2, swap_3, own_c,
    base_0, base_1, base_2, base_3, spread, out,
):
    place = lax.axis_index("elem")
    second = lax.axis_index("gust") == 1
    _, rows, total = masked.shape
    cut = rows // 2
    flips_of = range(total // rows)
    loads = (None, load_1, load_2, load_3)
    swaps = (None, swap_1, swap_2, swap_3)

    def flipped(values):
        odd = place % 2 == 1
        high = place // 2 == 1
        near = [jnp.where(odd, values[i ^ 1], values[i]) for i in flips_of]
        return [jnp.where(high, near[i ^ 2], near[i]) for i in flips_of]

    def rows_right(value):
        return jnp.where(second, pltpu.roll(value, cut, 1), value)

    def received(flip, start, count):
        columns = pl.ds(start, count)
        return jnp.concatenate([loads[flip][:, columns], swaps[flip][:, columns]], axis=0)

    def times(fresh_b, lag, flip):
        if flip == 0:
            return dot_rows(fresh_b, masked[lag])
        return rows_right(dot_rows(fresh_b, received(flip, lag * total, total)))

    def corrected(drive, flip):
        lhs = jnp.concatenate(words_of(drive, 2), axis=0)
        added = 0.0
        for word in range(2):
            if flip == 0:
                rhs = own_c[:, word * rows : (word + 1) * rows]
            else:
                rhs = received(flip, (LATE - 1) * total + word * rows, rows)
            both = dot_rows(lhs, rhs)
            added = added + (both[:GUST_ROWS] + both[GUST_ROWS:])
        return drive + (added if flip == 0 else rows_right(added))

    waiting = [[base[step] for base in (base_0, base_1, base_2, base_3)] for step in range(STEPS)]
    waiting[LATE] = waiting[LATE][:1]
    for step in range(LATE):
        fresh = [corrected(waiting[step][flip], flip) for flip in flips_of]
        out[step] = fresh[0]
        whole = jnp.concatenate(flipped(fresh), axis=1)
        fresh_b = whole.astype(jnp.bfloat16)
        slope = slope_of(whole, spread)
        slope = flipped([slope[:, i * rows : (i + 1) * rows] for i in flips_of])
        for later in range(step + 1, STEPS):
            lag = later - step - 1
            for flip in range(len(waiting[later])):
                change = times(fresh_b, lag, flip)
                if lag == 0:
                    change = change - slope[flip]
                waiting[later][flip] = waiting[later][flip] - change
    out[LATE] = corrected(waiting[LATE][0], 0)


def on_core(body, shapes, operands, scratch=(), in_specs=None, cost=(0, 0), name=None):
    vmem = pl.BlockSpec(memory_space=pltpu.VMEM)
    return pl.pallas_call(
        body,
        out_shape=[jax.ShapeDtypeStruct(shape, dtype) for shape, dtype in shapes],
        in_specs=in_specs or [vmem] * len(operands),
        out_specs=[vmem] * len(shapes),
        scratch_shapes=list(scratch),
        cost_estimate=pl.CostEstimate(flops=cost[0], bytes_accessed=cost[1], transcendentals=0),
        compiler_params=pltpu.CompilerParams(vmem_limit_bytes=24 * 2**20),
        name=name,
    )(*operands)


def places_march(history, forcing, interaction, block_mask, correction, neighbours, edge_coef):
    f32, bf16 = jnp.float32, jnp.bfloat16
    rows = correction.shape[0]
    lags, gusts, _ = history.shape
    total = rows * lax.axis_size("elem")
    part_rows = 24
    vmem = pl.BlockSpec(memory_space=pltpu.VMEM)
    smem = pl.BlockSpec(memory_space=pltpu.SMEM)

    (message,) = on_core(
        pack, [((64, rows), bf16)], (history, neighbours, edge_coef), name="pack"
    )
    messages = flips(message)
    masked, own_c, load = on_core(
        make_load,
        [
            (interaction.shape, bf16),
            ((rows, 2 * rows), bf16),
            ((rows // 2, (LATE - 1) * total + 2 * rows), bf16),
        ],
        (block_mask[:, 0, :], interaction, correction),
        in_specs=[smem, vmem, vmem],
        cost=(10**6, 3 * 2**20),
        name="load",
    )
    loads = flips(load)[1:]
    swaps = [lax.ppermute(piece, "gust", [(0, 1), (1, 0)]) for piece in loads]

    everyone, late = on_core(
        order, [((64, total), bf16), ((LATE * gusts, total), bf16)], messages, name="order"
    )
    before = lax.ppermute(late, "lag", [(0, 1), (1, 0)])
    part, slope, spread = on_core(
        main_part,
        [((part_rows, rows), f32), ((GUST_ROWS, rows), f32), ((2 * RIM, total), f32)],
        (everyone, masked),
        scratch=[pltpu.VMEM((56, total), f32), pltpu.VMEM((GUST_ROWS, total), f32)],
        cost=(10**7, 2**20),
        name="main_part",
    )
    (part,) = on_core(
        late_part,
        [((part_rows, rows), f32)],
        (before, masked, part),
        scratch=[pltpu.VMEM((40, total), f32)],
        name="late_part",
    )
    other = lax.ppermute(part, "lag", [(0, 1), (1, 0)])
    (base,) = on_core(
        make_base,
        [((STEPS, GUST_ROWS, rows), f32)],
        (part, other, forcing, slope),
        name="base",
    )
    bases = flips(base)
    (own,) = on_core(
        march,
        [((STEPS, GUST_ROWS, rows), f32)],
        (masked, *loads, *swaps, own_c, *bases, spread),
        cost=(10**8, 4 * 2**20),
        name="march",
    )
    moved = lax.ppermute(own, "lag", [(0, 1), (1, 0)])
    return jnp.where(lax.axis_index("lag") == 0, own, moved)[:, :gusts]


def solution(mesh):
    placed = (
        P("lag", ("groups", "gust"), "elem"),
        P(None, ("groups", "gust"), "elem"),
        P("lag", "elem", None),
        P("lag", "elem", None),
        P("elem", None),
        P(None, "elem"),
        P(None, "elem"),
    )
    small = mesh.shape["elem"] == 4 and mesh.shape["lag"] == 2 and mesh.shape["gust"] == 2
    return jax.shard_map(
        places_march if small else exchange_each_step,
        mesh=mesh,
        in_specs=placed,
        out_specs=P(None, ("groups", "gust"), "elem"),
        check_vma=False,
    )
```

```python
import jax
import jax.numpy as jnp
from jax import lax
from jax.experimental import pallas as pl
from jax.experimental.pallas import tpu as pltpu
from jax.sharding import PartitionSpec as P

RIM = 8
STEPS = 5
LATE = STEPS - 1
GUST_ROWS = 8


def flips(value, flipped=(1, 2, 3)):
    count = lax.axis_size("elem")
    return [value] + [
        lax.ppermute(value, "elem", [(i, i ^ flip) for i in range(count)]) for flip in flipped
    ]


def lag_behind(value):
    count = lax.axis_size("lag")
    moved = lax.ppermute(value, "lag", [(i, (i + 1) % count) for i in range(count)])
    return jnp.where(lax.axis_index("lag") == 0, jnp.zeros_like(moved), moved)


def by_offset(neighbours, edge_coef):
    rows = neighbours.shape[1]
    total = rows * lax.axis_size("elem")
    places = lax.axis_index("elem") * rows + jnp.arange(rows, dtype=jnp.int32)
    return (neighbours - places[None, :] + RIM) % total


def spread_weights(offsets, edge_coef):
    return [
        jnp.sum(jnp.where(offsets == d, edge_coef, 0.0), axis=0, keepdims=True)
        for d in range(2 * RIM + 1)
    ]


def own_gradient(newest, spread):
    rows = spread[0].shape[1]
    total = newest.shape[1]
    wide = jnp.concatenate([newest[:, total - RIM :], newest, newest[:, :RIM]], axis=1)
    start = lax.axis_index("elem") * rows
    window = lax.dynamic_slice(wide, (0, start), (newest.shape[0], rows + 2 * RIM))
    own = window[:, RIM : RIM + rows]
    out = jnp.zeros_like(own)
    for d in range(2 * RIM + 1):
        if d != RIM:
            out += spread[d] * (window[:, d : d + rows] - own)
    return out


def known_part(hist, masked):
    lags, gusts, total = hist.shape
    longer = jnp.concatenate([lag_behind(hist[lags - LATE :]), hist], axis=0)
    stacked = jnp.stack(
        [longer[LATE - step : LATE - step + lags] for step in range(STEPS)], axis=1
    ).reshape(lags, STEPS * gusts, total)
    part = jnp.einsum("lmc,lrc->mr", stacked, masked, preferred_element_type=jnp.float32)
    return part.reshape(STEPS, gusts, masked.shape[1])


def live_coefficients(interaction, block_mask, rows):
    live = jnp.repeat(block_mask[:, 0, :].astype(jnp.bfloat16), rows, axis=1)
    return interaction * live[:, None, :]


def exchange_each_step(
    history, forcing, interaction, block_mask, correction, neighbours, edge_coef
):
    rows = correction.shape[0]
    masked = live_coefficients(interaction, block_mask, rows)
    spread = spread_weights(by_offset(neighbours, edge_coef), edge_coef)

    def gathered(value, dim):
        return lax.all_gather(value, "elem", axis=dim, tiled=True)

    hist = gathered(history.astype(jnp.bfloat16), 2)
    newest = gathered(history[0], 1)
    base = forcing - lax.psum(known_part(hist, masked), "lag")
    fresh_b = []
    results = []
    for step in range(STEPS):
        drive = base[step] + own_gradient(newest, spread)
        if step:
            past = jnp.stack(fresh_b[::-1], axis=0)
            drive -= jnp.einsum(
                "lgc,lrc->gr", past, masked[:step], preferred_element_type=jnp.float32
            )
        fresh = drive + jnp.dot(drive, correction.T, precision=lax.Precision.HIGHEST)
        results.append(fresh)
        if step < LATE:
            newest = gathered(fresh, 1)
            fresh_b.append(newest.astype(jnp.bfloat16))
    first = lax.axis_index("lag") == 0
    return lax.psum(jnp.where(first, jnp.stack(results, 0), 0.0), "lag")


def dot_rows(lhs, rhs):
    return lax.dot_general(lhs, rhs, (((1,), (1,)), ((), ())), preferred_element_type=jnp.float32)


def words_of(value, count):
    out = []
    for _ in range(count):
        word = value.astype(jnp.bfloat16)
        out.append(word)
        value = value - word.astype(jnp.float32)
    return out


def fetched(copies, sems):
    started = [
        pltpu.make_async_copy(source, target, sems.at[index])
        for index, (source, target) in enumerate(copies)
    ]
    for copy in started:
        copy.start()
    for copy in started:
        copy.wait()


def pack(history_in, neighbours_in, edge_coef_in, message, history, neighbours, edge_coef, sems):
    fetched(
        [(history_in, history), (neighbours_in, neighbours), (edge_coef_in, edge_coef)], sems
    )
    lags, gusts, rows = history.shape
    total = rows * lax.axis_size("elem")
    places = lax.axis_index("elem") * rows + lax.broadcasted_iota(
        jnp.int32, neighbours.shape, 1
    )
    offsets = lax.rem(neighbours[...] - places + (RIM + total), total)
    pieces = [history[lag] for lag in range(lags)]
    _, mid, low = words_of(history[0], 3)
    pieces += [mid.astype(jnp.float32), low.astype(jnp.float32), offsets.astype(jnp.float32)]
    pieces += [word.astype(jnp.float32) for word in words_of(edge_coef[...], 3)]
    pieces += [jnp.zeros_like(pieces[0])] * (message.shape[0] // gusts - len(pieces))
    message[...] = jnp.concatenate(pieces, axis=0).astype(jnp.bfloat16)


def make_load(
    after, mask_in, interaction_in, correction_in, masked, own_c, near_load, mid_load,
    mask, interaction, correction, sems,
):
    del after
    fetched(
        [(mask_in, mask), (interaction_in, interaction), (correction_in, correction)], sems
    )
    lags, rows, total = interaction.shape
    blocks = total // rows
    cut = rows // 2
    for lag in range(lags):
        for block in range(blocks):
            columns = pl.ds(block * rows, rows)
            piece = interaction[lag, :, columns]
            live = mask[lag, 0, block] != 0
            masked[lag, :, columns] = jnp.where(live, piece, jnp.zeros_like(piece))
    own_c[...] = jnp.concatenate(words_of(correction[...], 2), axis=1)
    start = pl.multiple_of(lax.axis_index("gust") * cut, cut)
    places = [lag * total for lag in range(LATE - 1)] + [(LATE - 1) * total + 2 * rows]
    for lag, at in enumerate(places):
        near_load[:, pl.ds(at, total)] = masked[lag, pl.ds(start, cut), :]
    near_load[:, pl.ds((LATE - 1) * total, 2 * rows)] = own_c[pl.ds(start, cut), :]
    mid_load[...] = near_load[:, : mid_load.shape[1]]


def relay(after, near, load):
    del after
    load[...] = near[:, : load.shape[1]]


def all_spread(after, everyone, spread):
    del after
    gusts = 4
    known = everyone.shape[0] // 2

    def piece(index):
        at = known + index * gusts
        return everyone[at : at + gusts, :].astype(jnp.float32)

    offsets = piece(2)
    coef = piece(3) + (piece(4) + piece(5))
    for d in range(2 * RIM):
        value = d if d < RIM else d + 1
        spread[d : d + 1, :] = jnp.sum(
            jnp.where(offsets == float(value), coef, 0.0), axis=0, keepdims=True
        )


def order(piece_0, piece_1, piece_2, piece_3, everyone, late):
    place = lax.axis_index("elem")
    rows = piece_0.shape[1]
    for flip, piece in enumerate((piece_0, piece_1, piece_2, piece_3)):
        start = pl.multiple_of((place ^ flip) * rows, rows)
        everyone[:, pl.ds(start, rows)] = piece[...]
    late[...] = everyone[late.shape[0] : 2 * late.shape[0], :]


def slope_of(newest, spread_ref):
    total = newest.shape[1]
    out = jnp.zeros_like(newest)
    for d in range(2 * RIM):
        shift = d - RIM if d < RIM else d - RIM + 1
        moved = pltpu.roll(newest, (-shift) % total, 1)
        out += spread_ref[d : d + 1, :] * (moved - newest)
    return out


def main_part(everyone, masked, part, slope, longer, spread, slopes):
    lags, rows, total = masked.shape
    gusts = 4
    known = lags * gusts
    wide = everyone[...].astype(jnp.float32)
    longer[...] = jnp.zeros_like(longer)
    longer[LATE * gusts : LATE * gusts + known, :] = wide[:known]
    acc = jnp.zeros(part.shape, jnp.float32)
    for lag in range(lags):
        lhs = longer[lag * gusts : lag * gusts + part.shape[0], :].astype(jnp.bfloat16)
        acc += dot_rows(lhs, masked[lag])
    part[...] = acc

    def piece(index):
        return wide[known + index * gusts : known + (index + 1) * gusts]

    newest = wide[:gusts] + (piece(0) + piece(1))
    offsets = piece(2)
    coef = piece(3) + (piece(4) + piece(5))
    for d in range(2 * RIM):
        value = d if d < RIM else d + 1
        spread[d : d + 1, :] = jnp.sum(
            jnp.where(offsets == float(value), coef, 0.0), axis=0, keepdims=True
        )
    newest = jnp.concatenate([newest, jnp.zeros_like(newest)], axis=0)
    slopes[...] = slope_of(newest, spread)
    start = pl.multiple_of(lax.axis_index("elem") * rows, rows)
    slope[...] = slopes[:, pl.ds(start, rows)]


def late_part(late, masked, part, both, longer):
    gusts = late.shape[0] // LATE
    value = late[...].astype(jnp.float32)
    longer[...] = jnp.zeros_like(longer)
    longer[: late.shape[0], :] = jnp.where(lax.axis_index("lag") == 0, 0.0, value)
    acc = part[...]
    for lag in range(LATE):
        lhs = longer[lag * gusts : lag * gusts + part.shape[0], :].astype(jnp.bfloat16)
        acc += dot_rows(lhs, masked[lag])
    both[...] = acc


def known_base(part, forcing, slope, ahead):
    gusts = forcing.shape[1]
    for step in range(STEPS):
        at = (STEPS - 1 - step) * gusts
        value = forcing[step] - part[at : at + gusts, :]
        if step == 0:
            value = value + slope[:gusts, :]
        ahead[step] = jnp.concatenate([value, jnp.zeros_like(value)], axis=0)


def make_base(ahead, other, base):
    gusts = 4
    for step in range(STEPS):
        at = (STEPS - 1 - step) * gusts
        value = other[at : at + gusts, :]
        base[step] = ahead[step] - jnp.concatenate([value, jnp.zeros_like(value)], axis=0)


def march(
    masked, load_1, load_2, load_3, swap_1, swap_2, swap_3, own_c,
    base_0, base_1, base_2, base_3, spread, out, near_out,
):
    place = lax.axis_index("elem")
    second = lax.axis_index("gust") == 1
    _, rows, total = masked.shape
    cut = rows // 2
    flips_of = range(total // rows)
    loads = (None, load_1, load_2, load_3)
    swaps = (None, swap_1, swap_2, swap_3)

    def flipped(values):
        odd = place % 2 == 1
        high = place // 2 == 1
        near = [jnp.where(odd, values[i ^ 1], values[i]) for i in flips_of]
        return [jnp.where(high, near[i ^ 2], near[i]) for i in flips_of]

    def rows_right(value):
        return jnp.where(second, pltpu.roll(value, cut, 1), value)

    def received(flip, start, count):
        columns = pl.ds(start, count)
        return jnp.concatenate([loads[flip][:, columns], swaps[flip][:, columns]], axis=0)

    def times(fresh_b, lag, flip):
        if flip == 0:
            return dot_rows(fresh_b, masked[lag])
        at = lag * total + (2 * rows if lag == LATE - 1 else 0)
        return rows_right(dot_rows(fresh_b, received(flip, at, total)))

    def corrected(drive, flip):
        lhs = jnp.concatenate(words_of(drive, 2), axis=0)
        added = 0.0
        for word in range(2):
            if flip == 0:
                rhs = own_c[:, word * rows : (word + 1) * rows]
            else:
                rhs = received(flip, (LATE - 1) * total + word * rows, rows)
            both = dot_rows(lhs, rhs)
            added = added + (both[:GUST_ROWS] + both[GUST_ROWS:])
        return drive + (added if flip == 0 else rows_right(added))

    waiting = [[base[step] for base in (base_0, base_1, base_2, base_3)] for step in range(STEPS)]
    waiting[LATE] = waiting[LATE][:2]
    for step in range(LATE):
        fresh = [corrected(waiting[step][flip], flip) for flip in flips_of]
        out[step], near_out[step] = fresh[:2]
        whole = jnp.concatenate(flipped(fresh), axis=1)
        fresh_b = whole.astype(jnp.bfloat16)
        slope = slope_of(whole, spread)
        slope = flipped([slope[:, i * rows : (i + 1) * rows] for i in flips_of])
        for later in range(step + 1, STEPS):
            lag = later - step - 1
            for flip in range(len(waiting[later])):
                change = times(fresh_b, lag, flip)
                if lag == 0:
                    change = change - slope[flip]
                waiting[later][flip] = waiting[later][flip] - change
    out[LATE], near_out[LATE] = (corrected(waiting[LATE][flip], flip) for flip in (0, 1))


def on_core(body, shapes, operands, scratch=(), in_specs=None, limit=24, name=None):
    vmem = pl.BlockSpec(memory_space=pltpu.VMEM)
    return pl.pallas_call(
        body,
        out_shape=[jax.ShapeDtypeStruct(shape, dtype) for shape, dtype in shapes],
        in_specs=in_specs or [vmem] * len(operands),
        out_specs=[vmem] * len(shapes),
        scratch_shapes=list(scratch),
        cost_estimate=pl.CostEstimate(flops=0, bytes_accessed=2**26, transcendentals=0),
        compiler_params=pltpu.CompilerParams(vmem_limit_bytes=limit * 2**20 if limit else None),
        name=name,
    )(*operands)


def places_march(history, forcing, interaction, block_mask, correction, neighbours, edge_coef):
    f32, bf16 = jnp.float32, jnp.bfloat16
    rows = correction.shape[0]
    lags, gusts, _ = history.shape
    count = lax.axis_size("elem")
    total = rows * count
    part_rows = 24
    width = (LATE - 1) * total + 2 * rows
    anywhere = pl.BlockSpec(memory_space=pl.ANY)
    vmem = pl.BlockSpec(memory_space=pltpu.VMEM)

    def like(value):
        return pltpu.VMEM(value.shape, value.dtype)

    def crossed(value, axis):
        return lax.ppermute(value, axis, [(0, 1), (1, 0)])

    (message,) = on_core(
        pack,
        [((64, rows), bf16)],
        (history, neighbours, edge_coef),
        scratch=[like(history), like(neighbours), like(edge_coef), pltpu.SemaphoreType.DMA((3,))],
        in_specs=[anywhere] * 3,
        limit=None,
        name="pack",
    )
    messages = flips(message)
    masked, own_c, near_load, mid_load = on_core(
        make_load,
        [
            (interaction.shape, bf16),
            ((rows, 2 * rows), bf16),
            ((rows // 2, width + total), bf16),
            ((rows // 2, width), bf16),
        ],
        (message, block_mask, interaction, correction),
        scratch=[
            pltpu.SMEM(block_mask.shape, block_mask.dtype),
            like(interaction),
            like(correction),
            pltpu.SemaphoreType.DMA((3,)),
        ],
        in_specs=[anywhere] * 4,
        name="load",
    )
    everyone, late = on_core(
        order, [((64, total), bf16), ((LATE * gusts, total), bf16)], messages, name="order"
    )
    before = crossed(late, "lag")
    part, slope = on_core(
        main_part,
        [((part_rows, rows), f32), ((GUST_ROWS, rows), f32)],
        (everyone, masked),
        scratch=[
            pltpu.VMEM((56, total), f32),
            pltpu.VMEM((2 * RIM, total), f32),
            pltpu.VMEM((GUST_ROWS, total), f32),
        ],
        name="main_part",
    )

    near_load, mid_load, _ = lax.optimization_barrier((near_load, mid_load, slope))

    def bulk(value, pairs):
        return lax.ppermute(value, ("elem", "lag"), [(2 * a, 2 * b) for a, b in pairs])

    near = bulk(near_load, [(i, i ^ 1) for i in range(count)])
    mid = bulk(mid_load, [(1, 2), (2, 1)])

    (part,) = on_core(
        late_part,
        [((part_rows, rows), f32)],
        (before, masked, part),
        scratch=[pltpu.VMEM((40, total), f32)],
        name="late_part",
    )
    other = crossed(part, "lag")
    (ahead,) = on_core(
        known_base,
        [((STEPS, GUST_ROWS, rows), f32)],
        (part, forcing, slope),
        name="known_base",
    )
    (far_load,) = on_core(
        relay, [((rows // 2, width), bf16)], (ahead, near), in_specs=[anywhere, vmem], name="relay"
    )
    far = bulk(far_load, [(1, 2), (2, 1)])
    (base,) = on_core(
        make_base, [((STEPS, GUST_ROWS, rows), f32)], (ahead, other), name="base"
    )
    bases = flips(base)
    (spread,) = on_core(
        all_spread,
        [((2 * RIM, total), f32)],
        (base, everyone),
        in_specs=[anywhere, vmem],
        name="spread",
    )
    loads, _ = lax.optimization_barrier(((near, far, mid), spread))
    swaps = [crossed(piece, "gust") for piece in loads]
    own, outer = on_core(
        march,
        [((STEPS, GUST_ROWS, rows), f32)] * 2,
        (masked, *loads, *swaps, own_c, *bases, spread),
        name="march",
    )

    def swap(value, flip):
        return lax.ppermute(value, ("elem", "lag"), [(i, i ^ flip) for i in range(2 * count)])

    to_lag, to_outer, to_both = swap(own, 1), swap(outer, 2), swap(outer, 3)
    place = lax.axis_index("elem")
    middle = (place == 1) | (place == 2)
    first = lax.axis_index("lag") == 0
    result = jnp.where(
        middle, jnp.where(first, own, to_lag), jnp.where(first, to_outer, to_both)
    )
    return result[:, :gusts]


def solution(mesh):
    placed = (
        P("lag", ("groups", "gust"), "elem"),
        P(None, ("groups", "gust"), "elem"),
        P("lag", "elem", None),
        P("lag", "elem", None),
        P("elem", None),
        P(None, "elem"),
        P(None, "elem"),
    )
    small = mesh.shape["elem"] == 4 and mesh.shape["lag"] == 2 and mesh.shape["gust"] == 2
    return jax.shard_map(
        places_march if small else exchange_each_step,
        mesh=mesh,
        in_specs=placed,
        out_specs=P(None, ("groups", "gust"), "elem"),
        check_vma=False,
    )
```

```python
import jax
import jax.numpy as jnp
from jax import lax
from jax.experimental import pallas as pl
from jax.experimental.pallas import tpu as pltpu
from jax.sharding import PartitionSpec as P

RIM = 8
STEPS = 5
LATE = STEPS - 1
GUST_ROWS = 8


def flips(value, flipped=(1, 2, 3)):
    count = lax.axis_size("elem")
    return [value] + [
        lax.ppermute(value, "elem", [(i, i ^ flip) for i in range(count)]) for flip in flipped
    ]


def lag_behind(value):
    count = lax.axis_size("lag")
    moved = lax.ppermute(value, "lag", [(i, (i + 1) % count) for i in range(count)])
    return jnp.where(lax.axis_index("lag") == 0, jnp.zeros_like(moved), moved)


def by_offset(neighbours, edge_coef):
    rows = neighbours.shape[1]
    total = rows * lax.axis_size("elem")
    places = lax.axis_index("elem") * rows + jnp.arange(rows, dtype=jnp.int32)
    return (neighbours - places[None, :] + RIM) % total


def spread_weights(offsets, edge_coef):
    return [
        jnp.sum(jnp.where(offsets == d, edge_coef, 0.0), axis=0, keepdims=True)
        for d in range(2 * RIM + 1)
    ]


def own_gradient(newest, spread):
    rows = spread[0].shape[1]
    total = newest.shape[1]
    wide = jnp.concatenate([newest[:, total - RIM :], newest, newest[:, :RIM]], axis=1)
    start = lax.axis_index("elem") * rows
    window = lax.dynamic_slice(wide, (0, start), (newest.shape[0], rows + 2 * RIM))
    own = window[:, RIM : RIM + rows]
    out = jnp.zeros_like(own)
    for d in range(2 * RIM + 1):
        if d != RIM:
            out += spread[d] * (window[:, d : d + rows] - own)
    return out


def known_part(hist, masked):
    lags, gusts, total = hist.shape
    longer = jnp.concatenate([lag_behind(hist[lags - LATE :]), hist], axis=0)
    stacked = jnp.stack(
        [longer[LATE - step : LATE - step + lags] for step in range(STEPS)], axis=1
    ).reshape(lags, STEPS * gusts, total)
    part = jnp.einsum("lmc,lrc->mr", stacked, masked, preferred_element_type=jnp.float32)
    return part.reshape(STEPS, gusts, masked.shape[1])


def live_coefficients(interaction, block_mask, rows):
    live = jnp.repeat(block_mask[:, 0, :].astype(jnp.bfloat16), rows, axis=1)
    return interaction * live[:, None, :]


def exchange_each_step(
    history, forcing, interaction, block_mask, correction, neighbours, edge_coef
):
    rows = correction.shape[0]
    masked = live_coefficients(interaction, block_mask, rows)
    spread = spread_weights(by_offset(neighbours, edge_coef), edge_coef)

    def gathered(value, dim):
        return lax.all_gather(value, "elem", axis=dim, tiled=True)

    hist = gathered(history.astype(jnp.bfloat16), 2)
    newest = gathered(history[0], 1)
    base = forcing - lax.psum(known_part(hist, masked), "lag")
    fresh_b = []
    results = []
    for step in range(STEPS):
        drive = base[step] + own_gradient(newest, spread)
        if step:
            past = jnp.stack(fresh_b[::-1], axis=0)
            drive -= jnp.einsum(
                "lgc,lrc->gr", past, masked[:step], preferred_element_type=jnp.float32
            )
        fresh = drive + jnp.dot(drive, correction.T, precision=lax.Precision.HIGHEST)
        results.append(fresh)
        if step < LATE:
            newest = gathered(fresh, 1)
            fresh_b.append(newest.astype(jnp.bfloat16))
    first = lax.axis_index("lag") == 0
    return lax.psum(jnp.where(first, jnp.stack(results, 0), 0.0), "lag")


def dot_rows(lhs, rhs):
    return lax.dot_general(lhs, rhs, (((1,), (1,)), ((), ())), preferred_element_type=jnp.float32)


def words_of(value, count):
    out = []
    for _ in range(count):
        word = value.astype(jnp.bfloat16)
        out.append(word)
        value = value - word.astype(jnp.float32)
    return out


def fetched(copies, sems):
    started = [
        pltpu.make_async_copy(source, target, sems.at[index])
        for index, (source, target) in enumerate(copies)
    ]
    for copy in started:
        copy.start()
    for copy in started:
        copy.wait()


def pack(history_in, neighbours_in, edge_coef_in, message, history, neighbours, edge_coef, sems):
    fetched(
        [(history_in, history), (neighbours_in, neighbours), (edge_coef_in, edge_coef)], sems
    )
    lags, gusts, rows = history.shape
    total = rows * lax.axis_size("elem")
    places = lax.axis_index("elem") * rows + lax.broadcasted_iota(
        jnp.int32, neighbours.shape, 1
    )
    offsets = lax.rem(neighbours[...] - places + (RIM + total), total)
    pieces = [history[lag] for lag in range(lags)]
    _, mid, low = words_of(history[0], 3)
    pieces += [mid.astype(jnp.float32), low.astype(jnp.float32), offsets.astype(jnp.float32)]
    pieces += [word.astype(jnp.float32) for word in words_of(edge_coef[...], 3)]
    pieces += [jnp.zeros_like(pieces[0])] * (message.shape[0] // gusts - len(pieces))
    message[...] = jnp.concatenate(pieces, axis=0).astype(jnp.bfloat16)


def make_load(
    after, mask_in, interaction_in, correction_in, masked, own_c, near_load, mid_load,
    mask, interaction, correction, sems,
):
    del after
    fetched(
        [(mask_in, mask), (interaction_in, interaction), (correction_in, correction)], sems
    )
    lags, rows, total = interaction.shape
    blocks = total // rows
    cut = rows // 2
    for lag in range(lags):
        for block in range(blocks):
            columns = pl.ds(block * rows, rows)
            piece = interaction[lag, :, columns]
            live = mask[lag, 0, block] != 0
            masked[lag, :, columns] = jnp.where(live, piece, jnp.zeros_like(piece))
    own_c[...] = jnp.concatenate(words_of(correction[...], 2), axis=1)
    start = pl.multiple_of(lax.axis_index("gust") * cut, cut)
    places = [lag * total for lag in range(LATE - 1)] + [(LATE - 1) * total + 2 * rows]
    for lag, at in enumerate(places):
        near_load[:, pl.ds(at, total)] = masked[lag, pl.ds(start, cut), :]
    near_load[:, pl.ds((LATE - 1) * total, 2 * rows)] = own_c[pl.ds(start, cut), :]
    mid_load[...] = near_load[:, : mid_load.shape[1]]


def relay(after, near, load):
    del after
    load[...] = near[:, : load.shape[1]]


def all_spread(after, everyone, spread):
    del after
    gusts = 4
    known = everyone.shape[0] // 2

    def piece(index):
        at = known + index * gusts
        return everyone[at : at + gusts, :].astype(jnp.float32)

    offsets = piece(2)
    coef = piece(3) + (piece(4) + piece(5))
    for d in range(2 * RIM):
        value = d if d < RIM else d + 1
        spread[d : d + 1, :] = jnp.sum(
            jnp.where(offsets == float(value), coef, 0.0), axis=0, keepdims=True
        )


def order(piece_0, piece_1, piece_2, piece_3, everyone, late):
    place = lax.axis_index("elem")
    rows = piece_0.shape[1]
    for flip, piece in enumerate((piece_0, piece_1, piece_2, piece_3)):
        start = pl.multiple_of((place ^ flip) * rows, rows)
        everyone[:, pl.ds(start, rows)] = piece[...]
    late[...] = everyone[late.shape[0] : 2 * late.shape[0], :]


def slope_of(newest, spread_ref):
    total = newest.shape[1]
    out = jnp.zeros_like(newest)
    for d in range(2 * RIM):
        shift = d - RIM if d < RIM else d - RIM + 1
        moved = pltpu.roll(newest, (-shift) % total, 1)
        out += spread_ref[d : d + 1, :] * (moved - newest)
    return out


def main_part(everyone, masked, part, slope, longer, spread, slopes):
    lags, rows, total = masked.shape
    gusts = 4
    known = lags * gusts
    wide = everyone[...].astype(jnp.float32)
    longer[...] = jnp.zeros_like(longer)
    longer[LATE * gusts : LATE * gusts + known, :] = wide[:known]
    acc = jnp.zeros(part.shape, jnp.float32)
    for lag in range(lags):
        lhs = longer[lag * gusts : lag * gusts + part.shape[0], :].astype(jnp.bfloat16)
        acc += dot_rows(lhs, masked[lag])
    part[...] = acc

    def piece(index):
        return wide[known + index * gusts : known + (index + 1) * gusts]

    newest = wide[:gusts] + (piece(0) + piece(1))
    offsets = piece(2)
    coef = piece(3) + (piece(4) + piece(5))
    for d in range(2 * RIM):
        value = d if d < RIM else d + 1
        spread[d : d + 1, :] = jnp.sum(
            jnp.where(offsets == float(value), coef, 0.0), axis=0, keepdims=True
        )
    newest = jnp.concatenate([newest, jnp.zeros_like(newest)], axis=0)
    slopes[...] = slope_of(newest, spread)
    start = pl.multiple_of(lax.axis_index("elem") * rows, rows)
    slope[...] = slopes[:, pl.ds(start, rows)]


def late_part(late, masked, part, both, longer):
    gusts = late.shape[0] // LATE
    value = late[...].astype(jnp.float32)
    longer[...] = jnp.zeros_like(longer)
    longer[: late.shape[0], :] = jnp.where(lax.axis_index("lag") == 0, 0.0, value)
    acc = part[...]
    for lag in range(LATE):
        lhs = longer[lag * gusts : lag * gusts + part.shape[0], :].astype(jnp.bfloat16)
        acc += dot_rows(lhs, masked[lag])
    both[...] = acc


def known_base(part, forcing, slope, ahead):
    gusts = forcing.shape[1]
    for step in range(STEPS):
        at = (STEPS - 1 - step) * gusts
        value = forcing[step] - part[at : at + gusts, :]
        if step == 0:
            value = value + slope[:gusts, :]
        ahead[step] = jnp.concatenate([value, jnp.zeros_like(value)], axis=0)


def make_base(after, ahead, other, base):
    del after
    gusts = 4
    for step in range(STEPS):
        at = (STEPS - 1 - step) * gusts
        value = other[at : at + gusts, :]
        base[step] = ahead[step] - jnp.concatenate([value, jnp.zeros_like(value)], axis=0)


def march(
    masked, load_1, load_2, load_3, swap_1, swap_2, swap_3, own_c,
    base_0, base_1, base_2, base_3, spread, out, near_out,
):
    place = lax.axis_index("elem")
    second = lax.axis_index("gust") == 1
    _, rows, total = masked.shape
    cut = rows // 2
    flips_of = range(total // rows)
    loads = (None, load_1, load_2, load_3)
    swaps = (None, swap_1, swap_2, swap_3)

    def flipped(values):
        odd = place % 2 == 1
        high = place // 2 == 1
        near = [jnp.where(odd, values[i ^ 1], values[i]) for i in flips_of]
        return [jnp.where(high, near[i ^ 2], near[i]) for i in flips_of]

    def rows_right(value):
        return jnp.where(second, pltpu.roll(value, cut, 1), value)

    def received(flip, start, count):
        columns = pl.ds(start, count)
        return jnp.concatenate([loads[flip][:, columns], swaps[flip][:, columns]], axis=0)

    def times(fresh_b, lag, flip):
        if flip == 0:
            return dot_rows(fresh_b, masked[lag])
        at = lag * total + (2 * rows if lag == LATE - 1 else 0)
        return rows_right(dot_rows(fresh_b, received(flip, at, total)))

    def corrected(drive, flip):
        lhs = jnp.concatenate(words_of(drive, 2), axis=0)
        added = 0.0
        for word in range(2):
            if flip == 0:
                rhs = own_c[:, word * rows : (word + 1) * rows]
            else:
                rhs = received(flip, (LATE - 1) * total + word * rows, rows)
            both = dot_rows(lhs, rhs)
            added = added + (both[:GUST_ROWS] + both[GUST_ROWS:])
        return drive + (added if flip == 0 else rows_right(added))

    waiting = [[base[step] for base in (base_0, base_1, base_2, base_3)] for step in range(STEPS)]
    waiting[LATE] = waiting[LATE][:2]
    for step in range(LATE):
        fresh = [corrected(waiting[step][flip], flip) for flip in flips_of]
        out[step], near_out[step] = fresh[:2]
        whole = jnp.concatenate(flipped(fresh), axis=1)
        fresh_b = whole.astype(jnp.bfloat16)
        slope = slope_of(whole, spread)
        slope = flipped([slope[:, i * rows : (i + 1) * rows] for i in flips_of])
        for later in range(step + 1, STEPS):
            lag = later - step - 1
            for flip in range(len(waiting[later])):
                change = times(fresh_b, lag, flip)
                if lag == 0:
                    change = change - slope[flip]
                waiting[later][flip] = waiting[later][flip] - change
    out[LATE], near_out[LATE] = (corrected(waiting[LATE][flip], flip) for flip in (0, 1))


def on_core(body, shapes, operands, scratch=(), in_specs=None, limit=24, name=None):
    vmem = pl.BlockSpec(memory_space=pltpu.VMEM)
    return pl.pallas_call(
        body,
        out_shape=[jax.ShapeDtypeStruct(shape, dtype) for shape, dtype in shapes],
        in_specs=in_specs or [vmem] * len(operands),
        out_specs=[vmem] * len(shapes),
        scratch_shapes=list(scratch),
        cost_estimate=pl.CostEstimate(flops=10**10, bytes_accessed=2**20, transcendentals=0),
        compiler_params=pltpu.CompilerParams(vmem_limit_bytes=limit * 2**20 if limit else None),
        name=name,
    )(*operands)


def places_march(history, forcing, interaction, block_mask, correction, neighbours, edge_coef):
    f32, bf16 = jnp.float32, jnp.bfloat16
    rows = correction.shape[0]
    lags, gusts, _ = history.shape
    count = lax.axis_size("elem")
    total = rows * count
    part_rows = 24
    width = (LATE - 1) * total + 2 * rows
    anywhere = pl.BlockSpec(memory_space=pl.ANY)
    vmem = pl.BlockSpec(memory_space=pltpu.VMEM)

    def like(value):
        return pltpu.VMEM(value.shape, value.dtype)

    def crossed(value, axis):
        return lax.ppermute(value, axis, [(0, 1), (1, 0)])

    (message,) = on_core(
        pack,
        [((64, rows), bf16)],
        (history, neighbours, edge_coef),
        scratch=[like(history), like(neighbours), like(edge_coef), pltpu.SemaphoreType.DMA((3,))],
        in_specs=[anywhere] * 3,
        limit=None,
        name="pack",
    )
    messages = flips(message)
    masked, own_c, near_load, mid_load = on_core(
        make_load,
        [
            (interaction.shape, bf16),
            ((rows, 2 * rows), bf16),
            ((rows // 2, width + total), bf16),
            ((rows // 2, width), bf16),
        ],
        (message, block_mask, interaction, correction),
        scratch=[
            pltpu.SMEM(block_mask.shape, block_mask.dtype),
            like(interaction),
            like(correction),
            pltpu.SemaphoreType.DMA((3,)),
        ],
        in_specs=[anywhere] * 4,
        name="load",
    )
    everyone, late = on_core(
        order, [((64, total), bf16), ((LATE * gusts, total), bf16)], messages, name="order"
    )
    before = crossed(late, "lag")
    part, slope = on_core(
        main_part,
        [((part_rows, rows), f32), ((GUST_ROWS, rows), f32)],
        (everyone, masked),
        scratch=[
            pltpu.VMEM((56, total), f32),
            pltpu.VMEM((2 * RIM, total), f32),
            pltpu.VMEM((GUST_ROWS, total), f32),
        ],
        name="main_part",
    )

    mid_load, _ = lax.optimization_barrier((mid_load, slope))

    def bulk(value, pairs):
        return lax.ppermute(value, ("elem", "lag"), [(2 * a, 2 * b) for a, b in pairs])

    near = bulk(near_load, [(i, i ^ 1) for i in range(count)])
    mid = bulk(mid_load, [(1, 2), (2, 1)])

    (part,) = on_core(
        late_part,
        [((part_rows, rows), f32)],
        (before, masked, part),
        scratch=[pltpu.VMEM((40, total), f32)],
        name="late_part",
    )
    other = crossed(part, "lag")
    (ahead,) = on_core(
        known_base,
        [((STEPS, GUST_ROWS, rows), f32)],
        (part, forcing, slope),
        name="known_base",
    )
    (far_load,) = on_core(
        relay, [((rows // 2, width), bf16)], (ahead, near), in_specs=[anywhere, vmem], name="relay"
    )
    far = bulk(far_load, [(1, 2), (2, 1)])
    early, _ = lax.optimization_barrier(((near, mid), ahead))
    near_swap, mid_swap = (crossed(piece, "gust") for piece in early)
    (base,) = on_core(
        make_base,
        [((STEPS, GUST_ROWS, rows), f32)],
        (far_load, ahead, other),
        in_specs=[anywhere, vmem, vmem],
        name="base",
    )
    bases = flips(base)
    (spread,) = on_core(
        all_spread,
        [((2 * RIM, total), f32)],
        (base, everyone),
        in_specs=[anywhere, vmem],
        name="spread",
    )
    far, _ = lax.optimization_barrier((far, bases[3]))
    far_swap = crossed(far, "gust")
    own, outer = on_core(
        march,
        [((STEPS, GUST_ROWS, rows), f32)] * 2,
        (masked, near, far, mid, near_swap, far_swap, mid_swap, own_c, *bases, spread),
        name="march",
    )

    def swap(value, flip):
        return lax.ppermute(value, ("elem", "lag"), [(i, i ^ flip) for i in range(2 * count)])

    to_lag, to_outer, to_both = swap(own, 1), swap(outer, 2), swap(outer, 3)
    place = lax.axis_index("elem")
    middle = (place == 1) | (place == 2)
    first = lax.axis_index("lag") == 0
    result = jnp.where(
        middle, jnp.where(first, own, to_lag), jnp.where(first, to_outer, to_both)
    )
    return result[:, :gusts]


def solution(mesh):
    placed = (
        P("lag", ("groups", "gust"), "elem"),
        P(None, ("groups", "gust"), "elem"),
        P("lag", "elem", None),
        P("lag", "elem", None),
        P("elem", None),
        P(None, "elem"),
        P(None, "elem"),
    )
    small = mesh.shape["elem"] == 4 and mesh.shape["lag"] == 2 and mesh.shape["gust"] == 2
    return jax.shard_map(
        places_march if small else exchange_each_step,
        mesh=mesh,
        in_specs=placed,
        out_specs=P(None, ("groups", "gust"), "elem"),
        check_vma=False,
    )
```

```python
import jax
import jax.numpy as jnp
from jax import lax
from jax.experimental import pallas as pl
from jax.experimental.pallas import tpu as pltpu
from jax.sharding import PartitionSpec as P

RIM = 8
STEPS = 5
LATE = STEPS - 1
GUST_ROWS = 8
NEAR = ((0, 1), (1, 0), (2, 3), (3, 2))
MID = ((1, 2), (2, 1))
FAR = ((0, 2), (2, 0), (1, 3), (3, 1))


def flips(value, flipped=(1, 2, 3)):
    count = lax.axis_size("elem")
    return [value] + [
        lax.ppermute(value, "elem", [(i, i ^ flip) for i in range(count)]) for flip in flipped
    ]


def lag_behind(value):
    count = lax.axis_size("lag")
    moved = lax.ppermute(value, "lag", [(i, (i + 1) % count) for i in range(count)])
    return jnp.where(lax.axis_index("lag") == 0, jnp.zeros_like(moved), moved)


def by_offset(neighbours, edge_coef):
    rows = neighbours.shape[1]
    total = rows * lax.axis_size("elem")
    places = lax.axis_index("elem") * rows + jnp.arange(rows, dtype=jnp.int32)
    return (neighbours - places[None, :] + RIM) % total


def spread_weights(offsets, edge_coef):
    return [
        jnp.sum(jnp.where(offsets == d, edge_coef, 0.0), axis=0, keepdims=True)
        for d in range(2 * RIM + 1)
    ]


def own_gradient(newest, spread):
    rows = spread[0].shape[1]
    total = newest.shape[1]
    wide = jnp.concatenate([newest[:, total - RIM :], newest, newest[:, :RIM]], axis=1)
    start = lax.axis_index("elem") * rows
    window = lax.dynamic_slice(wide, (0, start), (newest.shape[0], rows + 2 * RIM))
    own = window[:, RIM : RIM + rows]
    out = jnp.zeros_like(own)
    for d in range(2 * RIM + 1):
        if d != RIM:
            out += spread[d] * (window[:, d : d + rows] - own)
    return out


def known_part(hist, masked):
    lags, gusts, total = hist.shape
    longer = jnp.concatenate([lag_behind(hist[lags - LATE :]), hist], axis=0)
    stacked = jnp.stack(
        [longer[LATE - step : LATE - step + lags] for step in range(STEPS)], axis=1
    ).reshape(lags, STEPS * gusts, total)
    part = jnp.einsum("lmc,lrc->mr", stacked, masked, preferred_element_type=jnp.float32)
    return part.reshape(STEPS, gusts, masked.shape[1])


def live_coefficients(interaction, block_mask, rows):
    live = jnp.repeat(block_mask[:, 0, :].astype(jnp.bfloat16), rows, axis=1)
    return interaction * live[:, None, :]


def exchange_each_step(
    history, forcing, interaction, block_mask, correction, neighbours, edge_coef
):
    rows = correction.shape[0]
    masked = live_coefficients(interaction, block_mask, rows)
    spread = spread_weights(by_offset(neighbours, edge_coef), edge_coef)

    def gathered(value, dim):
        return lax.all_gather(value, "elem", axis=dim, tiled=True)

    hist = gathered(history.astype(jnp.bfloat16), 2)
    newest = gathered(history[0], 1)
    base = forcing - lax.psum(known_part(hist, masked), "lag")
    fresh_b = []
    results = []
    for step in range(STEPS):
        drive = base[step] + own_gradient(newest, spread)
        if step:
            past = jnp.stack(fresh_b[::-1], axis=0)
            drive -= jnp.einsum(
                "lgc,lrc->gr", past, masked[:step], preferred_element_type=jnp.float32
            )
        fresh = drive + jnp.dot(drive, correction.T, precision=lax.Precision.HIGHEST)
        results.append(fresh)
        if step < LATE:
            newest = gathered(fresh, 1)
            fresh_b.append(newest.astype(jnp.bfloat16))
    first = lax.axis_index("lag") == 0
    return lax.psum(jnp.where(first, jnp.stack(results, 0), 0.0), "lag")


def dot_rows(lhs, rhs):
    return lax.dot_general(lhs, rhs, (((1,), (1,)), ((), ())), preferred_element_type=jnp.float32)


def words_of(value, count):
    out = []
    for _ in range(count):
        word = value.astype(jnp.bfloat16)
        out.append(word)
        value = value - word.astype(jnp.float32)
    return out


def fetched(copies, sems):
    started = [
        pltpu.make_async_copy(source, target, sems.at[index])
        for index, (source, target) in enumerate(copies)
    ]
    for copy in started:
        copy.start()
    for copy in started:
        copy.wait()


def pack(history_in, neighbours_in, edge_coef_in, message, history, neighbours, edge_coef, sems):
    fetched(
        [(history_in, history), (neighbours_in, neighbours), (edge_coef_in, edge_coef)], sems
    )
    lags, gusts, rows = history.shape
    total = rows * lax.axis_size("elem")
    places = lax.axis_index("elem") * rows + lax.broadcasted_iota(
        jnp.int32, neighbours.shape, 1
    )
    offsets = lax.rem(neighbours[...] - places + (RIM + total), total)
    pieces = [history[lag] for lag in range(lags)]
    _, mid, low = words_of(history[0], 3)
    pieces += [mid.astype(jnp.float32), low.astype(jnp.float32), offsets.astype(jnp.float32)]
    pieces += [word.astype(jnp.float32) for word in words_of(edge_coef[...], 3)]
    pieces += [jnp.zeros_like(pieces[0])] * (message.shape[0] // gusts - len(pieces))
    message[...] = jnp.concatenate(pieces, axis=0).astype(jnp.bfloat16)


def live_piece(interaction, mask, lag, block, columns, lines):
    piece = interaction[lag, lines, columns]
    return jnp.where(mask[0, block, lag] != 0, piece, jnp.zeros_like(piece))


def make_near_load(
    mask_in, interaction_in, correction_in, own_c, near_load, mask, interaction, correction, sems
):
    fetched(
        [
            (mask_in, mask),
            (interaction_in.at[pl.ds(0, LATE)], interaction),
            (correction_in, correction),
        ],
        sems,
    )
    _, rows, total = interaction.shape
    cut = rows // 2
    own_c[...] = jnp.concatenate(words_of(correction[...], 2), axis=1)
    start = pl.multiple_of(lax.axis_index("gust") * cut, cut)
    places = [lag * total for lag in range(LATE - 1)] + [(LATE - 1) * total + 2 * rows]
    for lag, at in enumerate(places):
        for block in range(total // rows):
            near_load[:, pl.ds(at + block * rows, rows)] = live_piece(
                interaction, mask, lag, block, pl.ds(block * rows, rows), pl.ds(start, cut)
            )
    near_load[:, pl.ds((LATE - 1) * total, 2 * rows)] = own_c[pl.ds(start, cut), :]


def make_masked(mask_in, interaction, near_load, masked, mid_load, mask, sems):
    fetched([(mask_in, mask)], sems)
    lags, rows, total = interaction.shape
    for lag in range(lags):
        for block in range(total // rows):
            columns = pl.ds(block * rows, rows)
            masked[lag, :, columns] = live_piece(
                interaction, mask, lag, block, columns, pl.ds(0, rows)
            )
    mid_load[...] = near_load[:, : mid_load.shape[1]]


def relay(after, near, load):
    del after
    load[...] = near[:, : load.shape[1]]


def all_spread(after, everyone, spread):
    del after
    gusts = 4
    known = everyone.shape[0] // 2

    def piece(index):
        at = known + index * gusts
        return everyone[at : at + gusts, :].astype(jnp.float32)

    offsets = piece(2)
    coef = piece(3) + (piece(4) + piece(5))
    for d in range(2 * RIM):
        value = d if d < RIM else d + 1
        spread[d : d + 1, :] = jnp.sum(
            jnp.where(offsets == float(value), coef, 0.0), axis=0, keepdims=True
        )


def order(piece_0, piece_1, piece_2, piece_3, everyone, late):
    place = lax.axis_index("elem")
    rows = piece_0.shape[1]
    for flip, piece in enumerate((piece_0, piece_1, piece_2, piece_3)):
        start = pl.multiple_of((place ^ flip) * rows, rows)
        everyone[:, pl.ds(start, rows)] = piece[...]
    late[...] = everyone[late.shape[0] : 2 * late.shape[0], :]


def slope_of(newest, spread_ref):
    total = newest.shape[1]
    out = jnp.zeros_like(newest)
    for d in range(2 * RIM):
        shift = d - RIM if d < RIM else d - RIM + 1
        moved = pltpu.roll(newest, (-shift) % total, 1)
        out += spread_ref[d : d + 1, :] * (moved - newest)
    return out


def main_part(everyone, masked, part, slope, longer, spread, slopes):
    lags, rows, total = masked.shape
    gusts = 4
    known = lags * gusts
    wide = everyone[...].astype(jnp.float32)
    longer[...] = jnp.zeros_like(longer)
    longer[LATE * gusts : LATE * gusts + known, :] = wide[:known]
    acc = jnp.zeros(part.shape, jnp.float32)
    for lag in range(lags):
        lhs = longer[lag * gusts : lag * gusts + part.shape[0], :].astype(jnp.bfloat16)
        acc += dot_rows(lhs, masked[lag])
    part[...] = acc

    def piece(index):
        return wide[known + index * gusts : known + (index + 1) * gusts]

    newest = wide[:gusts] + (piece(0) + piece(1))
    offsets = piece(2)
    coef = piece(3) + (piece(4) + piece(5))
    for d in range(2 * RIM):
        value = d if d < RIM else d + 1
        spread[d : d + 1, :] = jnp.sum(
            jnp.where(offsets == float(value), coef, 0.0), axis=0, keepdims=True
        )
    newest = jnp.concatenate([newest, jnp.zeros_like(newest)], axis=0)
    slopes[...] = slope_of(newest, spread)
    start = pl.multiple_of(lax.axis_index("elem") * rows, rows)
    slope[...] = slopes[:, pl.ds(start, rows)]


def late_part(late, masked, part, both, longer):
    gusts = late.shape[0] // LATE
    value = late[...].astype(jnp.float32)
    longer[...] = jnp.zeros_like(longer)
    longer[: late.shape[0], :] = jnp.where(lax.axis_index("lag") == 0, 0.0, value)
    acc = part[...]
    for lag in range(LATE):
        lhs = longer[lag * gusts : lag * gusts + part.shape[0], :].astype(jnp.bfloat16)
        acc += dot_rows(lhs, masked[lag])
    both[...] = acc


def known_base(part, forcing, slope, ahead):
    gusts = forcing.shape[1]
    for step in range(STEPS):
        at = (STEPS - 1 - step) * gusts
        value = forcing[step] - part[at : at + gusts, :]
        if step == 0:
            value = value + slope[:gusts, :]
        ahead[step] = jnp.concatenate([value, jnp.zeros_like(value)], axis=0)


def make_base(after, ahead, other, base):
    del after
    gusts = 4
    for step in range(STEPS):
        at = (STEPS - 1 - step) * gusts
        value = other[at : at + gusts, :]
        base[step] = ahead[step] - jnp.concatenate([value, jnp.zeros_like(value)], axis=0)


def march(
    masked, load_1, load_2, load_3, swap_1, swap_2, swap_3, own_c,
    base_0, base_1, base_2, base_3, spread, out, near_out,
):
    place = lax.axis_index("elem")
    second = lax.axis_index("gust") == 1
    _, rows, total = masked.shape
    cut = rows // 2
    flips_of = range(total // rows)
    loads = (None, load_1, load_2, load_3)
    swaps = (None, swap_1, swap_2, swap_3)

    def flipped(values):
        odd = place % 2 == 1
        high = place // 2 == 1
        near = [jnp.where(odd, values[i ^ 1], values[i]) for i in flips_of]
        return [jnp.where(high, near[i ^ 2], near[i]) for i in flips_of]

    def rows_right(value):
        return jnp.where(second, pltpu.roll(value, cut, 1), value)

    def received(flip, start, count):
        columns = pl.ds(start, count)
        return jnp.concatenate([loads[flip][:, columns], swaps[flip][:, columns]], axis=0)

    def times(fresh_b, lag, flip):
        if flip == 0:
            return dot_rows(fresh_b, masked[lag])
        at = lag * total + (2 * rows if lag == LATE - 1 else 0)
        return rows_right(dot_rows(fresh_b, received(flip, at, total)))

    def corrected(drive, flip):
        lhs = jnp.concatenate(words_of(drive, 2), axis=0)
        added = 0.0
        for word in range(2):
            if flip == 0:
                rhs = own_c[:, word * rows : (word + 1) * rows]
            else:
                rhs = received(flip, (LATE - 1) * total + word * rows, rows)
            both = dot_rows(lhs, rhs)
            added = added + (both[:GUST_ROWS] + both[GUST_ROWS:])
        return drive + (added if flip == 0 else rows_right(added))

    waiting = [[base[step] for base in (base_0, base_1, base_2, base_3)] for step in range(STEPS)]
    waiting[LATE] = waiting[LATE][:2]
    for step in range(LATE):
        fresh = [corrected(waiting[step][flip], flip) for flip in flips_of]
        out[step], near_out[step] = fresh[:2]
        whole = jnp.concatenate(flipped(fresh), axis=1)
        fresh_b = whole.astype(jnp.bfloat16)
        slope = slope_of(whole, spread)
        slope = flipped([slope[:, i * rows : (i + 1) * rows] for i in flips_of])
        for later in range(step + 1, STEPS):
            lag = later - step - 1
            for flip in range(len(waiting[later])):
                change = times(fresh_b, lag, flip)
                if lag == 0:
                    change = change - slope[flip]
                waiting[later][flip] = waiting[later][flip] - change
    out[LATE], near_out[LATE] = (corrected(waiting[LATE][flip], flip) for flip in (0, 1))


def on_core(body, shapes, operands, scratch=(), in_specs=None, limit=24, name=None):
    vmem = pl.BlockSpec(memory_space=pltpu.VMEM)
    return pl.pallas_call(
        body,
        out_shape=[jax.ShapeDtypeStruct(shape, dtype) for shape, dtype in shapes],
        in_specs=in_specs or [vmem] * len(operands),
        out_specs=[vmem] * len(shapes),
        scratch_shapes=list(scratch),
        cost_estimate=pl.CostEstimate(flops=10**10, bytes_accessed=2**20, transcendentals=0),
        compiler_params=pltpu.CompilerParams(vmem_limit_bytes=limit * 2**20 if limit else None),
        name=name,
    )(*operands)


def exchanged(value, pairs, count):
    named = {source for source, _ in pairs}
    moves = [(2 * a + core, 2 * b + core) for a, b in pairs for core in (0, 1)]
    moves += [
        (2 * i + core, 2 * i + 1 - core) for i in range(count) if i not in named for core in (0, 1)
    ]
    return lax.ppermute(value, ("elem", "lag", "gust"), moves)


def places_march(history, forcing, interaction, block_mask, correction, neighbours, edge_coef):
    f32, bf16 = jnp.float32, jnp.bfloat16
    rows = correction.shape[0]
    lags, gusts, _ = history.shape
    count = lax.axis_size("elem")
    total = rows * count
    part_rows = 24
    width = (LATE - 1) * total + 2 * rows
    anywhere = pl.BlockSpec(memory_space=pl.ANY)
    vmem = pl.BlockSpec(memory_space=pltpu.VMEM)

    def like(value):
        return pltpu.VMEM(value.shape, value.dtype)

    def crossed(value, axis):
        return lax.ppermute(value, axis, [(0, 1), (1, 0)])

    (message,) = on_core(
        pack,
        [((64, rows), bf16)],
        (history, neighbours, edge_coef),
        scratch=[like(history), like(neighbours), like(edge_coef), pltpu.SemaphoreType.DMA((3,))],
        in_specs=[anywhere] * 3,
        limit=None,
        name="pack",
    )
    messages = flips(message)
    mask = jnp.transpose(block_mask, (1, 2, 0))
    after_message, _ = lax.optimization_barrier((correction, message))
    own_c, near_load = on_core(
        make_near_load,
        [((rows, 2 * rows), bf16), ((rows // 2, width + total), bf16)],
        (mask, interaction, after_message),
        scratch=[
            pltpu.SMEM(mask.shape, mask.dtype),
            pltpu.VMEM((LATE, rows, total), bf16),
            like(correction),
            pltpu.SemaphoreType.DMA((3,)),
        ],
        in_specs=[anywhere] * 3,
        name="near_load",
    )
    masked, mid_load = on_core(
        make_masked,
        [(interaction.shape, bf16), ((rows // 2, width), bf16)],
        (mask, interaction, near_load),
        scratch=[pltpu.SMEM(mask.shape, mask.dtype), pltpu.SemaphoreType.DMA((1,))],
        in_specs=[anywhere, vmem, vmem],
        name="masked",
    )
    everyone, late = on_core(
        order, [((64, total), bf16), ((LATE * gusts, total), bf16)], messages, name="order"
    )
    before = crossed(late, "lag")
    part, slope = on_core(
        main_part,
        [((part_rows, rows), f32), ((GUST_ROWS, rows), f32)],
        (everyone, masked),
        scratch=[
            pltpu.VMEM((56, total), f32),
            pltpu.VMEM((2 * RIM, total), f32),
            pltpu.VMEM((GUST_ROWS, total), f32),
        ],
        name="main_part",
    )

    mid_load, _ = lax.optimization_barrier((mid_load, slope))

    def bulk(value, pairs):
        return exchanged(value, [(2 * a, 2 * b) for a, b in pairs], 2 * count)

    near = bulk(near_load, NEAR)
    mid = bulk(mid_load, MID)

    (part,) = on_core(
        late_part,
        [((part_rows, rows), f32)],
        (before, masked, part),
        scratch=[pltpu.VMEM((40, total), f32)],
        name="late_part",
    )
    other = crossed(part, "lag")
    (ahead,) = on_core(
        known_base,
        [((STEPS, GUST_ROWS, rows), f32)],
        (part, forcing, slope),
        name="known_base",
    )
    (far_load,) = on_core(
        relay, [((rows // 2, width), bf16)], (ahead, near), in_specs=[anywhere, vmem], name="relay"
    )
    far = bulk(far_load, MID)
    early, _ = lax.optimization_barrier(((near, mid), ahead))
    near_swap, mid_swap = (crossed(piece, "gust") for piece in early)
    (base,) = on_core(
        make_base,
        [((STEPS, GUST_ROWS, rows), f32)],
        (far_load, ahead, other),
        in_specs=[anywhere, vmem, vmem],
        name="base",
    )
    bases = [base] + [bulk(base, pairs) for pairs in (NEAR, FAR, MID)]
    (spread,) = on_core(
        all_spread,
        [((2 * RIM, total), f32)],
        (base, everyone),
        in_specs=[anywhere, vmem],
        name="spread",
    )
    far, _ = lax.optimization_barrier((far, bases[3]))
    far_swap = crossed(far, "gust")
    own, outer = on_core(
        march,
        [((STEPS, GUST_ROWS, rows), f32)] * 2,
        (masked, near, far, mid, near_swap, far_swap, mid_swap, own_c, *bases, spread),
        name="march",
    )

    def swap(value, to_elem, to_lag):
        pairs = [(2 * a, 2 * (a ^ to_elem) + to_lag) for a in (1, 2)]
        return exchanged(value, pairs + [(b, a) for a, b in pairs], 2 * count)

    to_both, to_outer, to_lag = swap(outer, 1, 1), swap(outer, 1, 0), swap(own, 0, 1)
    place = lax.axis_index("elem")
    middle = (place == 1) | (place == 2)
    first = lax.axis_index("lag") == 0
    result = jnp.where(
        middle, jnp.where(first, own, to_lag), jnp.where(first, to_outer, to_both)
    )
    return result[:, :gusts]


def solution(mesh):
    placed = (
        P("lag", ("groups", "gust"), "elem"),
        P(None, ("groups", "gust"), "elem"),
        P("lag", "elem", None),
        P("lag", "elem", None),
        P("elem", None),
        P(None, "elem"),
        P(None, "elem"),
    )
    small = mesh.shape["elem"] == 4 and mesh.shape["lag"] == 2 and mesh.shape["gust"] == 2
    return jax.shard_map(
        places_march if small else exchange_each_step,
        mesh=mesh,
        in_specs=placed,
        out_specs=P(None, ("groups", "gust"), "elem"),
        check_vma=False,
    )
```

```python
import jax
import jax.numpy as jnp
from jax import lax
from jax.experimental import pallas as pl
from jax.experimental.pallas import tpu as pltpu
from jax.sharding import PartitionSpec as P

RIM = 8
STEPS = 5
LATE = STEPS - 1
GUST_ROWS = 8
NEAR = ((0, 1), (1, 0), (2, 3), (3, 2))
MID = ((1, 2), (2, 1))
FAR = ((0, 2), (2, 0), (1, 3), (3, 1))


def flips(value, flipped=(1, 2, 3)):
    count = lax.axis_size("elem")
    return [value] + [
        lax.ppermute(value, "elem", [(i, i ^ flip) for i in range(count)]) for flip in flipped
    ]


def lag_behind(value):
    count = lax.axis_size("lag")
    moved = lax.ppermute(value, "lag", [(i, (i + 1) % count) for i in range(count)])
    return jnp.where(lax.axis_index("lag") == 0, jnp.zeros_like(moved), moved)


def by_offset(neighbours, edge_coef):
    rows = neighbours.shape[1]
    total = rows * lax.axis_size("elem")
    places = lax.axis_index("elem") * rows + jnp.arange(rows, dtype=jnp.int32)
    return (neighbours - places[None, :] + RIM) % total


def spread_weights(offsets, edge_coef):
    return [
        jnp.sum(jnp.where(offsets == d, edge_coef, 0.0), axis=0, keepdims=True)
        for d in range(2 * RIM + 1)
    ]


def own_gradient(newest, spread):
    rows = spread[0].shape[1]
    total = newest.shape[1]
    wide = jnp.concatenate([newest[:, total - RIM :], newest, newest[:, :RIM]], axis=1)
    start = lax.axis_index("elem") * rows
    window = lax.dynamic_slice(wide, (0, start), (newest.shape[0], rows + 2 * RIM))
    own = window[:, RIM : RIM + rows]
    out = jnp.zeros_like(own)
    for d in range(2 * RIM + 1):
        if d != RIM:
            out += spread[d] * (window[:, d : d + rows] - own)
    return out


def known_part(hist, masked):
    lags, gusts, total = hist.shape
    longer = jnp.concatenate([lag_behind(hist[lags - LATE :]), hist], axis=0)
    stacked = jnp.stack(
        [longer[LATE - step : LATE - step + lags] for step in range(STEPS)], axis=1
    ).reshape(lags, STEPS * gusts, total)
    part = jnp.einsum("lmc,lrc->mr", stacked, masked, preferred_element_type=jnp.float32)
    return part.reshape(STEPS, gusts, masked.shape[1])


def live_coefficients(interaction, block_mask, rows):
    live = jnp.repeat(block_mask[:, 0, :].astype(jnp.bfloat16), rows, axis=1)
    return interaction * live[:, None, :]


def exchange_each_step(
    history, forcing, interaction, block_mask, correction, neighbours, edge_coef
):
    rows = correction.shape[0]
    masked = live_coefficients(interaction, block_mask, rows)
    spread = spread_weights(by_offset(neighbours, edge_coef), edge_coef)

    def gathered(value, dim):
        return lax.all_gather(value, "elem", axis=dim, tiled=True)

    hist = gathered(history.astype(jnp.bfloat16), 2)
    newest = gathered(history[0], 1)
    base = forcing - lax.psum(known_part(hist, masked), "lag")
    fresh_b = []
    results = []
    for step in range(STEPS):
        drive = base[step] + own_gradient(newest, spread)
        if step:
            past = jnp.stack(fresh_b[::-1], axis=0)
            drive -= jnp.einsum(
                "lgc,lrc->gr", past, masked[:step], preferred_element_type=jnp.float32
            )
        fresh = drive + jnp.dot(drive, correction.T, precision=lax.Precision.HIGHEST)
        results.append(fresh)
        if step < LATE:
            newest = gathered(fresh, 1)
            fresh_b.append(newest.astype(jnp.bfloat16))
    first = lax.axis_index("lag") == 0
    return lax.psum(jnp.where(first, jnp.stack(results, 0), 0.0), "lag")


def dot_rows(lhs, rhs):
    return lax.dot_general(lhs, rhs, (((1,), (1,)), ((), ())), preferred_element_type=jnp.float32)


def words_of(value, count):
    out = []
    for _ in range(count):
        word = value.astype(jnp.bfloat16)
        out.append(word)
        value = value - word.astype(jnp.float32)
    return out


def fetched(copies, sems):
    started = [
        pltpu.make_async_copy(source, target, sems.at[index])
        for index, (source, target) in enumerate(copies)
    ]
    for copy in started:
        copy.start()
    for copy in started:
        copy.wait()


def pack(history_in, neighbours_in, edge_coef_in, message, history, neighbours, edge_coef, sems):
    fetched(
        [(history_in, history), (neighbours_in, neighbours), (edge_coef_in, edge_coef)], sems
    )
    lags, gusts, rows = history.shape
    total = rows * lax.axis_size("elem")
    places = lax.axis_index("elem") * rows + lax.broadcasted_iota(
        jnp.int32, neighbours.shape, 1
    )
    offsets = lax.rem(neighbours[...] - places + (RIM + total), total)
    pieces = [history[lag] for lag in range(lags)]
    _, mid, low = words_of(history[0], 3)
    pieces += [mid.astype(jnp.float32), low.astype(jnp.float32), offsets.astype(jnp.float32)]
    pieces += [word.astype(jnp.float32) for word in words_of(edge_coef[...], 3)]
    pieces += [jnp.zeros_like(pieces[0])] * (message.shape[0] // gusts - len(pieces))
    message[...] = jnp.concatenate(pieces, axis=0).astype(jnp.bfloat16)


def live_piece(interaction, mask, lag, block, columns, lines):
    piece = interaction[lag, lines, columns]
    return jnp.where(mask[0, block, lag] != 0, piece, jnp.zeros_like(piece))


def make_near_load(
    mask_in, interaction_in, correction_in, own_c, near_load, mask, interaction, correction, sems
):
    fetched(
        [
            (mask_in, mask),
            (interaction_in.at[pl.ds(0, LATE)], interaction),
            (correction_in, correction),
        ],
        sems,
    )
    _, rows, total = interaction.shape
    cut = rows // 2
    own_c[...] = jnp.concatenate(words_of(correction[...], 2), axis=1)
    start = pl.multiple_of(lax.axis_index("gust") * cut, cut)
    places = [lag * total for lag in range(LATE - 1)] + [(LATE - 1) * total + 2 * rows]
    for lag, at in enumerate(places):
        for block in range(total // rows):
            near_load[:, pl.ds(at + block * rows, rows)] = live_piece(
                interaction, mask, lag, block, pl.ds(block * rows, rows), pl.ds(start, cut)
            )
    near_load[:, pl.ds((LATE - 1) * total, 2 * rows)] = own_c[pl.ds(start, cut), :]


def make_masked(mask_in, interaction, near_load, masked, mid_load, mask, sems):
    fetched([(mask_in, mask)], sems)
    lags, rows, total = interaction.shape
    for lag in range(lags):
        for block in range(total // rows):
            columns = pl.ds(block * rows, rows)
            masked[lag, :, columns] = live_piece(
                interaction, mask, lag, block, columns, pl.ds(0, rows)
            )
    mid_load[...] = near_load[:, : mid_load.shape[1]]


def relay(after, near, load):
    del after
    load[...] = near[:, : load.shape[1]]


def all_spread(after, everyone, spread):
    del after
    gusts = 4
    known = everyone.shape[0] // 2

    def piece(index):
        at = known + index * gusts
        return everyone[at : at + gusts, :].astype(jnp.float32)

    offsets = piece(2)
    coef = piece(3) + (piece(4) + piece(5))
    for d in range(2 * RIM):
        value = d if d < RIM else d + 1
        spread[d : d + 1, :] = jnp.sum(
            jnp.where(offsets == float(value), coef, 0.0), axis=0, keepdims=True
        )


def order(piece_0, piece_2, piece_3, piece_1, everyone, late):
    place = lax.axis_index("elem")
    rows = piece_0.shape[1]
    for flip, piece in enumerate((piece_0, piece_1, piece_2, piece_3)):
        start = pl.multiple_of((place ^ flip) * rows, rows)
        everyone[:, pl.ds(start, rows)] = piece[...]
    late[...] = everyone[late.shape[0] : 2 * late.shape[0], :]


def slope_of(newest, spread_ref):
    total = newest.shape[1]
    out = jnp.zeros_like(newest)
    for d in range(2 * RIM):
        shift = d - RIM if d < RIM else d - RIM + 1
        moved = pltpu.roll(newest, (-shift) % total, 1)
        out += spread_ref[d : d + 1, :] * (moved - newest)
    return out


def main_part(everyone, masked, part, slope, longer, spread, slopes):
    lags, rows, total = masked.shape
    gusts = 4
    known = lags * gusts
    wide = everyone[...].astype(jnp.float32)
    longer[...] = jnp.zeros_like(longer)
    longer[LATE * gusts : LATE * gusts + known, :] = wide[:known]
    acc = jnp.zeros(part.shape, jnp.float32)
    for lag in range(lags):
        lhs = longer[lag * gusts : lag * gusts + part.shape[0], :].astype(jnp.bfloat16)
        acc += dot_rows(lhs, masked[lag])
    part[...] = acc

    def piece(index):
        return wide[known + index * gusts : known + (index + 1) * gusts]

    newest = wide[:gusts] + (piece(0) + piece(1))
    offsets = piece(2)
    coef = piece(3) + (piece(4) + piece(5))
    for d in range(2 * RIM):
        value = d if d < RIM else d + 1
        spread[d : d + 1, :] = jnp.sum(
            jnp.where(offsets == float(value), coef, 0.0), axis=0, keepdims=True
        )
    newest = jnp.concatenate([newest, jnp.zeros_like(newest)], axis=0)
    slopes[...] = slope_of(newest, spread)
    start = pl.multiple_of(lax.axis_index("elem") * rows, rows)
    slope[...] = slopes[:, pl.ds(start, rows)]


def late_part(late, masked, part, both, longer):
    gusts = late.shape[0] // LATE
    value = late[...].astype(jnp.float32)
    longer[...] = jnp.zeros_like(longer)
    longer[: late.shape[0], :] = jnp.where(lax.axis_index("lag") == 0, 0.0, value)
    acc = part[...]
    for lag in range(LATE):
        lhs = longer[lag * gusts : lag * gusts + part.shape[0], :].astype(jnp.bfloat16)
        acc += dot_rows(lhs, masked[lag])
    both[...] = acc


def known_base(part, forcing, slope, ahead):
    gusts = forcing.shape[1]
    for step in range(STEPS):
        at = (STEPS - 1 - step) * gusts
        value = forcing[step] - part[at : at + gusts, :]
        if step == 0:
            value = value + slope[:gusts, :]
        ahead[step] = jnp.concatenate([value, jnp.zeros_like(value)], axis=0)


def make_base(after, ahead, other, base):
    del after
    gusts = 4
    for step in range(STEPS):
        at = (STEPS - 1 - step) * gusts
        value = other[at : at + gusts, :]
        base[step] = ahead[step] - jnp.concatenate([value, jnp.zeros_like(value)], axis=0)


def march(
    masked, load_1, load_2, load_3, swap_1, swap_2, swap_3, own_c,
    base_0, base_1, base_2, base_3, spread, out, near_out,
):
    place = lax.axis_index("elem")
    second = lax.axis_index("gust") == 1
    _, rows, total = masked.shape
    cut = rows // 2
    flips_of = range(total // rows)
    loads = (None, load_1, load_2, load_3)
    swaps = (None, swap_1, swap_2, swap_3)

    def flipped(values):
        odd = place % 2 == 1
        high = place // 2 == 1
        near = [jnp.where(odd, values[i ^ 1], values[i]) for i in flips_of]
        return [jnp.where(high, near[i ^ 2], near[i]) for i in flips_of]

    def rows_right(value):
        return jnp.where(second, pltpu.roll(value, cut, 1), value)

    def received(flip, start, count):
        columns = pl.ds(start, count)
        return jnp.concatenate([loads[flip][:, columns], swaps[flip][:, columns]], axis=0)

    def times(fresh_b, lag, flip):
        if flip == 0:
            return dot_rows(fresh_b, masked[lag])
        at = lag * total + (2 * rows if lag == LATE - 1 else 0)
        return rows_right(dot_rows(fresh_b, received(flip, at, total)))

    def corrected(drive, flip):
        lhs = jnp.concatenate(words_of(drive, 2), axis=0)
        added = 0.0
        for word in range(2):
            if flip == 0:
                rhs = own_c[:, word * rows : (word + 1) * rows]
            else:
                rhs = received(flip, (LATE - 1) * total + word * rows, rows)
            both = dot_rows(lhs, rhs)
            added = added + (both[:GUST_ROWS] + both[GUST_ROWS:])
        return drive + (added if flip == 0 else rows_right(added))

    waiting = [[base[step] for base in (base_0, base_1, base_2, base_3)] for step in range(STEPS)]
    waiting[LATE] = waiting[LATE][:2]
    for step in range(LATE):
        fresh = [corrected(waiting[step][flip], flip) for flip in flips_of]
        out[step], near_out[step] = fresh[:2]
        whole = jnp.concatenate(flipped(fresh), axis=1)
        fresh_b = whole.astype(jnp.bfloat16)
        slope = slope_of(whole, spread)
        slope = flipped([slope[:, i * rows : (i + 1) * rows] for i in flips_of])
        for later in range(step + 1, STEPS):
            lag = later - step - 1
            for flip in range(len(waiting[later])):
                change = times(fresh_b, lag, flip)
                if lag == 0:
                    change = change - slope[flip]
                waiting[later][flip] = waiting[later][flip] - change
    out[LATE], near_out[LATE] = (corrected(waiting[LATE][flip], flip) for flip in (0, 1))


def on_core(body, shapes, operands, scratch=(), in_specs=None, limit=24, name=None, force=False):
    vmem = pl.BlockSpec(memory_space=pltpu.VMEM)
    return pl.pallas_call(
        body,
        out_shape=[
            pltpu.VMEM(shape, dtype) if force else jax.ShapeDtypeStruct(shape, dtype)
            for shape, dtype in shapes
        ],
        in_specs=in_specs or [vmem] * len(operands),
        out_specs=[vmem] * len(shapes),
        scratch_shapes=list(scratch),
        cost_estimate=pl.CostEstimate(flops=10**10, bytes_accessed=2**20, transcendentals=0),
        compiler_params=pltpu.CompilerParams(vmem_limit_bytes=limit * 2**20 if limit else None),
        name=name,
    )(*operands)


def exchanged(value, pairs, count):
    named = {source for source, _ in pairs}
    moves = [(2 * a + core, 2 * b + core) for a, b in pairs for core in (0, 1)]
    moves += [
        (2 * i + core, 2 * i + 1 - core) for i in range(count) if i not in named for core in (0, 1)
    ]
    return lax.ppermute(value, ("elem", "lag", "gust"), moves)


def places_march(history, forcing, interaction, block_mask, correction, neighbours, edge_coef):
    f32, bf16 = jnp.float32, jnp.bfloat16
    rows = correction.shape[0]
    lags, gusts, _ = history.shape
    count = lax.axis_size("elem")
    total = rows * count
    part_rows = 24
    width = (LATE - 1) * total + 2 * rows
    anywhere = pl.BlockSpec(memory_space=pl.ANY)
    vmem = pl.BlockSpec(memory_space=pltpu.VMEM)

    def like(value):
        return pltpu.VMEM(value.shape, value.dtype)

    def crossed(value, axis):
        return lax.ppermute(value, axis, [(0, 1), (1, 0)])

    (message,) = on_core(
        pack,
        [((64, rows), bf16)],
        (history, neighbours, edge_coef),
        scratch=[like(history), like(neighbours), like(edge_coef), pltpu.SemaphoreType.DMA((3,))],
        in_specs=[anywhere] * 3,
        limit=None,
        force=True,
        name="pack",
    )
    messages = flips(message)
    mask = jnp.transpose(block_mask, (1, 2, 0))
    after_message, _ = lax.optimization_barrier((correction, message))
    own_c, near_load = on_core(
        make_near_load,
        [((rows, 2 * rows), bf16), ((rows // 2, width + total), bf16)],
        (mask, interaction, after_message),
        scratch=[
            pltpu.SMEM(mask.shape, mask.dtype),
            pltpu.VMEM((LATE, rows, total), bf16),
            like(correction),
            pltpu.SemaphoreType.DMA((3,)),
        ],
        in_specs=[anywhere] * 3,
        name="near_load",
    )
    masked, mid_load = on_core(
        make_masked,
        [(interaction.shape, bf16), ((rows // 2, width), bf16)],
        (mask, interaction, near_load),
        scratch=[pltpu.SMEM(mask.shape, mask.dtype), pltpu.SemaphoreType.DMA((1,))],
        in_specs=[anywhere, vmem, vmem],
        name="masked",
    )
    everyone, late = on_core(
        order,
        [((64, total), bf16), ((LATE * gusts, total), bf16)],
        [messages[flip] for flip in (0, 2, 3, 1)],
        name="order",
    )
    before = crossed(late, "lag")
    part, slope = on_core(
        main_part,
        [((part_rows, rows), f32), ((GUST_ROWS, rows), f32)],
        (everyone, masked),
        scratch=[
            pltpu.VMEM((56, total), f32),
            pltpu.VMEM((2 * RIM, total), f32),
            pltpu.VMEM((GUST_ROWS, total), f32),
        ],
        name="main_part",
    )

    mid_load, _ = lax.optimization_barrier((mid_load, slope))

    def bulk(value, pairs):
        return exchanged(value, [(2 * a, 2 * b) for a, b in pairs], 2 * count)

    near = bulk(near_load, NEAR)
    mid = bulk(mid_load, MID)

    (part,) = on_core(
        late_part,
        [((part_rows, rows), f32)],
        (before, masked, part),
        scratch=[pltpu.VMEM((40, total), f32)],
        name="late_part",
    )
    other = crossed(part, "lag")
    (ahead,) = on_core(
        known_base,
        [((STEPS, GUST_ROWS, rows), f32)],
        (part, forcing, slope),
        name="known_base",
    )
    (far_load,) = on_core(
        relay, [((rows // 2, width), bf16)], (ahead, near), in_specs=[anywhere, vmem], name="relay"
    )
    far = bulk(far_load, MID)
    early, _ = lax.optimization_barrier(((near, mid), ahead))
    near_swap, mid_swap = (crossed(piece, "gust") for piece in early)
    (base,) = on_core(
        make_base,
        [((STEPS, GUST_ROWS, rows), f32)],
        (far_load, ahead, other),
        in_specs=[anywhere, vmem, vmem],
        name="base",
    )
    bases = [base] + [bulk(base, pairs) for pairs in (NEAR, FAR, MID)]
    (spread,) = on_core(
        all_spread,
        [((2 * RIM, total), f32)],
        (base, everyone),
        in_specs=[anywhere, vmem],
        name="spread",
    )
    far, _ = lax.optimization_barrier((far, bases[3]))
    far_swap = crossed(far, "gust")
    own, outer = on_core(
        march,
        [((STEPS, GUST_ROWS, rows), f32)] * 2,
        (masked, near, far, mid, near_swap, far_swap, mid_swap, own_c, *bases, spread),
        name="march",
    )

    def handed(value, *cycles):
        moves = []
        for cycle in cycles:
            moves += zip(cycle, cycle[1:] + cycle[:1])
        return exchanged(value, moves, 2 * count)

    to_both = handed(outer, [2, 1, 3], [4, 7, 5])
    to_outer = handed(outer, [2, 0], [4, 6])
    to_lag = handed(own, [2, 3], [4, 5])
    place = lax.axis_index("elem")
    inside = (place == 1) | (place == 2)
    first = lax.axis_index("lag") == 0
    result = jnp.where(
        inside, jnp.where(first, own, to_lag), jnp.where(first, to_outer, to_both)
    )
    return result[:, :gusts]


def solution(mesh):
    placed = (
        P("lag", ("groups", "gust"), "elem"),
        P(None, ("groups", "gust"), "elem"),
        P("lag", "elem", None),
        P("lag", "elem", None),
        P("elem", None),
        P(None, "elem"),
        P(None, "elem"),
    )
    small = mesh.shape["elem"] == 4 and mesh.shape["lag"] == 2 and mesh.shape["gust"] == 2
    return jax.shard_map(
        places_march if small else exchange_each_step,
        mesh=mesh,
        in_specs=placed,
        out_specs=P(None, ("groups", "gust"), "elem"),
        check_vma=False,
    )
```

```python
import jax
import jax.numpy as jnp
from jax import lax
from jax.experimental import pallas as pl
from jax.experimental.pallas import tpu as pltpu
from jax.sharding import PartitionSpec as P

RIM = 8
STEPS = 5
LATE = STEPS - 1
GUST_ROWS = 8
NEAR = ((0, 1), (1, 0), (2, 3), (3, 2))
MID = ((1, 2), (2, 1))
FAR = ((0, 2), (2, 0), (1, 3), (3, 1))


def flips(value, flipped=(1, 2, 3)):
    count = lax.axis_size("elem")
    return [value] + [
        lax.ppermute(value, "elem", [(i, i ^ flip) for i in range(count)]) for flip in flipped
    ]


def lag_behind(value):
    count = lax.axis_size("lag")
    moved = lax.ppermute(value, "lag", [(i, (i + 1) % count) for i in range(count)])
    return jnp.where(lax.axis_index("lag") == 0, jnp.zeros_like(moved), moved)


def by_offset(neighbours, edge_coef):
    rows = neighbours.shape[1]
    total = rows * lax.axis_size("elem")
    places = lax.axis_index("elem") * rows + jnp.arange(rows, dtype=jnp.int32)
    return (neighbours - places[None, :] + RIM) % total


def spread_weights(offsets, edge_coef):
    return [
        jnp.sum(jnp.where(offsets == d, edge_coef, 0.0), axis=0, keepdims=True)
        for d in range(2 * RIM + 1)
    ]


def own_gradient(newest, spread):
    rows = spread[0].shape[1]
    total = newest.shape[1]
    wide = jnp.concatenate([newest[:, total - RIM :], newest, newest[:, :RIM]], axis=1)
    start = lax.axis_index("elem") * rows
    window = lax.dynamic_slice(wide, (0, start), (newest.shape[0], rows + 2 * RIM))
    own = window[:, RIM : RIM + rows]
    out = jnp.zeros_like(own)
    for d in range(2 * RIM + 1):
        if d != RIM:
            out += spread[d] * (window[:, d : d + rows] - own)
    return out


def known_part(hist, masked):
    lags, gusts, total = hist.shape
    longer = jnp.concatenate([lag_behind(hist[lags - LATE :]), hist], axis=0)
    stacked = jnp.stack(
        [longer[LATE - step : LATE - step + lags] for step in range(STEPS)], axis=1
    ).reshape(lags, STEPS * gusts, total)
    part = jnp.einsum("lmc,lrc->mr", stacked, masked, preferred_element_type=jnp.float32)
    return part.reshape(STEPS, gusts, masked.shape[1])


def live_coefficients(interaction, block_mask, rows):
    live = jnp.repeat(block_mask[:, 0, :].astype(jnp.bfloat16), rows, axis=1)
    return interaction * live[:, None, :]


def exchange_each_step(
    history, forcing, interaction, block_mask, correction, neighbours, edge_coef
):
    rows = correction.shape[0]
    masked = live_coefficients(interaction, block_mask, rows)
    spread = spread_weights(by_offset(neighbours, edge_coef), edge_coef)

    def gathered(value, dim):
        return lax.all_gather(value, "elem", axis=dim, tiled=True)

    hist = gathered(history.astype(jnp.bfloat16), 2)
    newest = gathered(history[0], 1)
    base = forcing - lax.psum(known_part(hist, masked), "lag")
    fresh_b = []
    results = []
    for step in range(STEPS):
        drive = base[step] + own_gradient(newest, spread)
        if step:
            past = jnp.stack(fresh_b[::-1], axis=0)
            drive -= jnp.einsum(
                "lgc,lrc->gr", past, masked[:step], preferred_element_type=jnp.float32
            )
        fresh = drive + jnp.dot(drive, correction.T, precision=lax.Precision.HIGHEST)
        results.append(fresh)
        if step < LATE:
            newest = gathered(fresh, 1)
            fresh_b.append(newest.astype(jnp.bfloat16))
    first = lax.axis_index("lag") == 0
    return lax.psum(jnp.where(first, jnp.stack(results, 0), 0.0), "lag")


def dot_rows(lhs, rhs):
    return lax.dot_general(lhs, rhs, (((1,), (1,)), ((), ())), preferred_element_type=jnp.float32)


def words_of(value, count):
    out = []
    for _ in range(count):
        word = value.astype(jnp.bfloat16)
        out.append(word)
        value = value - word.astype(jnp.float32)
    return out


def fetched(copies, sems):
    started = [
        pltpu.make_async_copy(source, target, sems.at[index])
        for index, (source, target) in enumerate(copies)
    ]
    for copy in started:
        copy.start()
    for copy in started:
        copy.wait()


def pack(history_in, neighbours_in, edge_coef_in, message, history, neighbours, edge_coef, sems):
    fetched(
        [(history_in, history), (neighbours_in, neighbours), (edge_coef_in, edge_coef)], sems
    )
    lags, gusts, rows = history.shape
    total = rows * lax.axis_size("elem")
    places = lax.axis_index("elem") * rows + lax.broadcasted_iota(
        jnp.int32, neighbours.shape, 1
    )
    offsets = lax.rem(neighbours[...] - places + (RIM + total), total)
    pieces = [history[lag] for lag in range(lags)]
    _, mid, low = words_of(history[0], 3)
    pieces += [mid.astype(jnp.float32), low.astype(jnp.float32), offsets.astype(jnp.float32)]
    pieces += [word.astype(jnp.float32) for word in words_of(edge_coef[...], 3)]
    pieces += [jnp.zeros_like(pieces[0])] * (message.shape[0] // gusts - len(pieces))
    message[...] = jnp.concatenate(pieces, axis=0).astype(jnp.bfloat16)


def live_piece(interaction, mask, lag, block, columns, lines):
    piece = interaction[lag, lines, columns]
    return jnp.where(mask[0, block, lag] != 0, piece, jnp.zeros_like(piece))


def make_near_load(
    mask_in, interaction_in, correction_in, own_c, near_load, mask, interaction, correction, sems
):
    fetched(
        [
            (mask_in, mask),
            (interaction_in.at[pl.ds(0, LATE)], interaction),
            (correction_in, correction),
        ],
        sems,
    )
    _, rows, total = interaction.shape
    cut = rows // 2
    own_c[...] = jnp.concatenate(words_of(correction[...], 2), axis=1)
    start = pl.multiple_of(lax.axis_index("gust") * cut, cut)
    places = [lag * total for lag in range(LATE - 1)] + [(LATE - 1) * total + 2 * rows]
    for lag, at in enumerate(places):
        for block in range(total // rows):
            near_load[:, pl.ds(at + block * rows, rows)] = live_piece(
                interaction, mask, lag, block, pl.ds(block * rows, rows), pl.ds(start, cut)
            )
    near_load[:, pl.ds((LATE - 1) * total, 2 * rows)] = own_c[pl.ds(start, cut), :]


def make_masked(mask_in, interaction, near_load, masked, mid_load, mask, sems):
    fetched([(mask_in, mask)], sems)
    lags, rows, total = interaction.shape
    for lag in range(lags):
        for block in range(total // rows):
            columns = pl.ds(block * rows, rows)
            masked[lag, :, columns] = live_piece(
                interaction, mask, lag, block, columns, pl.ds(0, rows)
            )
    mid_load[...] = near_load[:, : mid_load.shape[1]]


def relay(after, near, load):
    del after
    load[...] = near[:, : load.shape[1]]


def all_spread(after, everyone, spread):
    del after
    gusts = 4
    known = everyone.shape[0] // 2

    def piece(index):
        at = known + index * gusts
        return everyone[at : at + gusts, :].astype(jnp.float32)

    offsets = piece(2)
    coef = piece(3) + (piece(4) + piece(5))
    for d in range(2 * RIM):
        value = d if d < RIM else d + 1
        spread[d : d + 1, :] = jnp.sum(
            jnp.where(offsets == float(value), coef, 0.0), axis=0, keepdims=True
        )


def order(piece_0, piece_2, piece_3, piece_1, everyone, late):
    place = lax.axis_index("elem")
    rows = piece_0.shape[1]
    for flip, piece in enumerate((piece_0, piece_1, piece_2, piece_3)):
        start = pl.multiple_of((place ^ flip) * rows, rows)
        everyone[:, pl.ds(start, rows)] = piece[...]
    late[...] = everyone[late.shape[0] : 2 * late.shape[0], :]


def slope_of(newest, spread_ref):
    total = newest.shape[1]
    out = jnp.zeros_like(newest)
    for d in range(2 * RIM):
        shift = d - RIM if d < RIM else d - RIM + 1
        moved = pltpu.roll(newest, (-shift) % total, 1)
        out += spread_ref[d : d + 1, :] * (moved - newest)
    return out


def main_part(everyone, masked, part, slope, longer, spread, slopes):
    lags, rows, total = masked.shape
    gusts = 4
    known = lags * gusts
    wide = everyone[...].astype(jnp.float32)
    longer[...] = jnp.zeros_like(longer)
    longer[LATE * gusts : LATE * gusts + known, :] = wide[:known]
    acc = jnp.zeros(part.shape, jnp.float32)
    for lag in range(lags):
        lhs = longer[lag * gusts : lag * gusts + part.shape[0], :].astype(jnp.bfloat16)
        acc += dot_rows(lhs, masked[lag])
    part[...] = acc

    def piece(index):
        return wide[known + index * gusts : known + (index + 1) * gusts]

    newest = wide[:gusts] + (piece(0) + piece(1))
    offsets = piece(2)
    coef = piece(3) + (piece(4) + piece(5))
    for d in range(2 * RIM):
        value = d if d < RIM else d + 1
        spread[d : d + 1, :] = jnp.sum(
            jnp.where(offsets == float(value), coef, 0.0), axis=0, keepdims=True
        )
    newest = jnp.concatenate([newest, jnp.zeros_like(newest)], axis=0)
    slopes[...] = slope_of(newest, spread)
    start = pl.multiple_of(lax.axis_index("elem") * rows, rows)
    slope[...] = slopes[:, pl.ds(start, rows)]


def late_part(late, masked, part, both, longer):
    gusts = late.shape[0] // LATE
    value = late[...].astype(jnp.float32)
    longer[...] = jnp.zeros_like(longer)
    longer[: late.shape[0], :] = jnp.where(lax.axis_index("lag") == 0, 0.0, value)
    acc = part[...]
    for lag in range(LATE):
        lhs = longer[lag * gusts : lag * gusts + part.shape[0], :].astype(jnp.bfloat16)
        acc += dot_rows(lhs, masked[lag])
    both[...] = acc


def known_base(part, forcing, slope, ahead):
    gusts = forcing.shape[1]
    for step in range(STEPS):
        at = (STEPS - 1 - step) * gusts
        value = forcing[step] - part[at : at + gusts, :]
        if step == 0:
            value = value + slope[:gusts, :]
        ahead[step] = jnp.concatenate([value, jnp.zeros_like(value)], axis=0)


def make_base(after, ahead, other, base):
    del after
    gusts = 4
    for step in range(STEPS):
        at = (STEPS - 1 - step) * gusts
        value = other[at : at + gusts, :]
        base[step] = ahead[step] - jnp.concatenate([value, jnp.zeros_like(value)], axis=0)


def march(
    masked, load_1, load_2, load_3, swap_1, swap_2, swap_3, own_c,
    base_0, base_1, base_2, base_3, spread, out, near_out,
):
    place = lax.axis_index("elem")
    second = lax.axis_index("gust") == 1
    _, rows, total = masked.shape
    cut = rows // 2
    flips_of = range(total // rows)
    loads = (None, load_1, load_2, load_3)
    swaps = (None, swap_1, swap_2, swap_3)

    def flipped(values):
        odd = place % 2 == 1
        high = place // 2 == 1
        near = [jnp.where(odd, values[i ^ 1], values[i]) for i in flips_of]
        return [jnp.where(high, near[i ^ 2], near[i]) for i in flips_of]

    def rows_right(value):
        return jnp.where(second, pltpu.roll(value, cut, 1), value)

    def received(flip, start, count):
        columns = pl.ds(start, count)
        return jnp.concatenate([loads[flip][:, columns], swaps[flip][:, columns]], axis=0)

    def times(fresh_b, lag, flip):
        if flip == 0:
            return dot_rows(fresh_b, masked[lag])
        at = lag * total + (2 * rows if lag == LATE - 1 else 0)
        return rows_right(dot_rows(fresh_b, received(flip, at, total)))

    def corrected(drive, flip):
        lhs = jnp.concatenate(words_of(drive, 2), axis=0)
        added = 0.0
        for word in range(2):
            if flip == 0:
                rhs = own_c[:, word * rows : (word + 1) * rows]
            else:
                rhs = received(flip, (LATE - 1) * total + word * rows, rows)
            both = dot_rows(lhs, rhs)
            added = added + (both[:GUST_ROWS] + both[GUST_ROWS:])
        return drive + (added if flip == 0 else rows_right(added))

    waiting = [[base[step] for base in (base_0, base_1, base_2, base_3)] for step in range(STEPS)]
    waiting[LATE] = waiting[LATE][:2]
    for step in range(LATE):
        fresh = [corrected(waiting[step][flip], flip) for flip in flips_of]
        out[step], near_out[step] = fresh[:2]
        whole = jnp.concatenate(flipped(fresh), axis=1)
        fresh_b = whole.astype(jnp.bfloat16)
        slope = slope_of(whole, spread)
        slope = flipped([slope[:, i * rows : (i + 1) * rows] for i in flips_of])
        for later in range(step + 1, STEPS):
            lag = later - step - 1
            for flip in range(len(waiting[later])):
                change = times(fresh_b, lag, flip)
                if lag == 0:
                    change = change - slope[flip]
                waiting[later][flip] = waiting[later][flip] - change
    out[LATE], near_out[LATE] = (corrected(waiting[LATE][flip], flip) for flip in (0, 1))


def on_core(body, shapes, operands, scratch=(), in_specs=None, limit=24, name=None, force=False):
    vmem = pl.BlockSpec(memory_space=pltpu.VMEM)
    return pl.pallas_call(
        body,
        out_shape=[
            pltpu.VMEM(shape, dtype) if force else jax.ShapeDtypeStruct(shape, dtype)
            for shape, dtype in shapes
        ],
        in_specs=in_specs or [vmem] * len(operands),
        out_specs=[vmem] * len(shapes),
        scratch_shapes=list(scratch),
        cost_estimate=pl.CostEstimate(flops=10**10, bytes_accessed=2**20, transcendentals=0),
        compiler_params=pltpu.CompilerParams(vmem_limit_bytes=limit * 2**20 if limit else None),
        name=name,
    )(*operands)


def exchanged(value, pairs, count):
    named = {source for source, _ in pairs}
    moves = [(2 * a + core, 2 * b + core) for a, b in pairs for core in (0, 1)]
    moves += [
        (2 * i + core, 2 * i + 1 - core) for i in range(count) if i not in named for core in (0, 1)
    ]
    return lax.ppermute(value, ("elem", "lag", "gust"), moves)


def places_march(history, forcing, interaction, block_mask, correction, neighbours, edge_coef):
    f32, bf16 = jnp.float32, jnp.bfloat16
    rows = correction.shape[0]
    lags, gusts, _ = history.shape
    count = lax.axis_size("elem")
    total = rows * count
    part_rows = 24
    width = (LATE - 1) * total + 2 * rows
    anywhere = pl.BlockSpec(memory_space=pl.ANY)
    vmem = pl.BlockSpec(memory_space=pltpu.VMEM)

    def like(value):
        return pltpu.VMEM(value.shape, value.dtype)

    def crossed(value, axis):
        return lax.ppermute(value, axis, [(0, 1), (1, 0)])

    (message,) = on_core(
        pack,
        [((64, rows), bf16)],
        (history, neighbours, edge_coef),
        scratch=[like(history), like(neighbours), like(edge_coef), pltpu.SemaphoreType.DMA((3,))],
        in_specs=[anywhere] * 3,
        limit=None,
        force=True,
        name="pack",
    )
    messages = flips(message)
    mask = jnp.transpose(block_mask, (1, 2, 0))
    after_message, _ = lax.optimization_barrier((correction, message))
    own_c, near_load = on_core(
        make_near_load,
        [((rows, 2 * rows), bf16), ((rows // 2, width + total), bf16)],
        (mask, interaction, after_message),
        scratch=[
            pltpu.SMEM(mask.shape, mask.dtype),
            pltpu.VMEM((LATE, rows, total), bf16),
            like(correction),
            pltpu.SemaphoreType.DMA((3,)),
        ],
        in_specs=[anywhere] * 3,
        name="near_load",
    )
    masked, mid_load = on_core(
        make_masked,
        [(interaction.shape, bf16), ((rows // 2, width), bf16)],
        (mask, interaction, near_load),
        scratch=[pltpu.SMEM(mask.shape, mask.dtype), pltpu.SemaphoreType.DMA((1,))],
        in_specs=[anywhere, vmem, vmem],
        name="masked",
    )
    everyone, late = on_core(
        order,
        [((64, total), bf16), ((LATE * gusts, total), bf16)],
        [messages[flip] for flip in (0, 2, 3, 1)],
        name="order",
    )
    before = crossed(late, "lag")
    part, slope = on_core(
        main_part,
        [((part_rows, rows), f32), ((GUST_ROWS, rows), f32)],
        (everyone, masked),
        scratch=[
            pltpu.VMEM((56, total), f32),
            pltpu.VMEM((2 * RIM, total), f32),
            pltpu.VMEM((GUST_ROWS, total), f32),
        ],
        name="main_part",
    )

    mid_load, _ = lax.optimization_barrier((mid_load, own_c))

    def bulk(value, pairs):
        return exchanged(value, [(2 * a, 2 * b) for a, b in pairs], 2 * count)

    near = bulk(near_load, NEAR)
    mid = bulk(mid_load, MID)

    (part,) = on_core(
        late_part,
        [((part_rows, rows), f32)],
        (before, masked, part),
        scratch=[pltpu.VMEM((40, total), f32)],
        name="late_part",
    )
    other = crossed(part, "lag")
    (ahead,) = on_core(
        known_base,
        [((STEPS, GUST_ROWS, rows), f32)],
        (part, forcing, slope),
        name="known_base",
    )
    (far_load,) = on_core(
        relay, [((rows // 2, width), bf16)], (ahead, near), in_specs=[anywhere, vmem], name="relay"
    )
    far = bulk(far_load, MID)
    early, _ = lax.optimization_barrier(((near, mid), ahead))
    near_swap, mid_swap = (crossed(piece, "gust") for piece in early)
    (base,) = on_core(
        make_base,
        [((STEPS, GUST_ROWS, rows), f32)],
        (far_load, ahead, other),
        in_specs=[anywhere, vmem, vmem],
        name="base",
    )
    bases = [base] + [bulk(base, pairs) for pairs in (NEAR, FAR, MID)]
    (spread,) = on_core(
        all_spread,
        [((2 * RIM, total), f32)],
        (base, everyone),
        in_specs=[anywhere, vmem],
        name="spread",
    )
    far, _ = lax.optimization_barrier((far, bases[3]))
    far_swap = crossed(far, "gust")
    own, outer = on_core(
        march,
        [((STEPS, GUST_ROWS, rows), f32)] * 2,
        (masked, near, far, mid, near_swap, far_swap, mid_swap, own_c, *bases, spread),
        name="march",
    )

    def handed(value, *cycles):
        moves = []
        for cycle in cycles:
            moves += zip(cycle, cycle[1:] + cycle[:1])
        return exchanged(value, moves, 2 * count)

    to_both = handed(outer, [2, 1, 3], [4, 7, 5])
    to_outer = handed(outer, [2, 0], [4, 6])
    to_lag = handed(own, [2, 3], [4, 5])
    place = lax.axis_index("elem")
    inside = (place == 1) | (place == 2)
    first = lax.axis_index("lag") == 0
    result = jnp.where(
        inside, jnp.where(first, own, to_lag), jnp.where(first, to_outer, to_both)
    )
    return result[:, :gusts]


def solution(mesh):
    placed = (
        P("lag", ("groups", "gust"), "elem"),
        P(None, ("groups", "gust"), "elem"),
        P("lag", "elem", None),
        P("lag", "elem", None),
        P("elem", None),
        P(None, "elem"),
        P(None, "elem"),
    )
    small = mesh.shape["elem"] == 4 and mesh.shape["lag"] == 2 and mesh.shape["gust"] == 2
    return jax.shard_map(
        places_march if small else exchange_each_step,
        mesh=mesh,
        in_specs=placed,
        out_specs=P(None, ("groups", "gust"), "elem"),
        check_vma=False,
    )
```

```python
import jax
import jax.numpy as jnp
from jax import lax
from jax.experimental import pallas as pl
from jax.experimental.pallas import tpu as pltpu
from jax.sharding import PartitionSpec as P

RIM = 8
STEPS = 5
LATE = STEPS - 1
GUST_ROWS = 8
NEAR = ((0, 1), (1, 0), (2, 3), (3, 2))
MID = ((1, 2), (2, 1))
FAR = ((0, 2), (2, 0), (1, 3), (3, 1))


def flips(value, flipped=(1, 2, 3)):
    count = lax.axis_size("elem")
    return [value] + [
        lax.ppermute(value, "elem", [(i, i ^ flip) for i in range(count)]) for flip in flipped
    ]


def lag_behind(value):
    count = lax.axis_size("lag")
    moved = lax.ppermute(value, "lag", [(i, (i + 1) % count) for i in range(count)])
    return jnp.where(lax.axis_index("lag") == 0, jnp.zeros_like(moved), moved)


def by_offset(neighbours, edge_coef):
    rows = neighbours.shape[1]
    total = rows * lax.axis_size("elem")
    places = lax.axis_index("elem") * rows + jnp.arange(rows, dtype=jnp.int32)
    return (neighbours - places[None, :] + RIM) % total


def spread_weights(offsets, edge_coef):
    return [
        jnp.sum(jnp.where(offsets == d, edge_coef, 0.0), axis=0, keepdims=True)
        for d in range(2 * RIM + 1)
    ]


def own_gradient(newest, spread):
    rows = spread[0].shape[1]
    total = newest.shape[1]
    wide = jnp.concatenate([newest[:, total - RIM :], newest, newest[:, :RIM]], axis=1)
    start = lax.axis_index("elem") * rows
    window = lax.dynamic_slice(wide, (0, start), (newest.shape[0], rows + 2 * RIM))
    own = window[:, RIM : RIM + rows]
    out = jnp.zeros_like(own)
    for d in range(2 * RIM + 1):
        if d != RIM:
            out += spread[d] * (window[:, d : d + rows] - own)
    return out


def known_part(hist, masked):
    lags, gusts, total = hist.shape
    longer = jnp.concatenate([lag_behind(hist[lags - LATE :]), hist], axis=0)
    stacked = jnp.stack(
        [longer[LATE - step : LATE - step + lags] for step in range(STEPS)], axis=1
    ).reshape(lags, STEPS * gusts, total)
    part = jnp.einsum("lmc,lrc->mr", stacked, masked, preferred_element_type=jnp.float32)
    return part.reshape(STEPS, gusts, masked.shape[1])


def live_coefficients(interaction, block_mask, rows):
    live = jnp.repeat(block_mask[:, 0, :].astype(jnp.bfloat16), rows, axis=1)
    return interaction * live[:, None, :]


def exchange_each_step(
    history, forcing, interaction, block_mask, correction, neighbours, edge_coef
):
    rows = correction.shape[0]
    masked = live_coefficients(interaction, block_mask, rows)
    spread = spread_weights(by_offset(neighbours, edge_coef), edge_coef)

    def gathered(value, dim):
        return lax.all_gather(value, "elem", axis=dim, tiled=True)

    hist = gathered(history.astype(jnp.bfloat16), 2)
    newest = gathered(history[0], 1)
    base = forcing - lax.psum(known_part(hist, masked), "lag")
    fresh_b = []
    results = []
    for step in range(STEPS):
        drive = base[step] + own_gradient(newest, spread)
        if step:
            past = jnp.stack(fresh_b[::-1], axis=0)
            drive -= jnp.einsum(
                "lgc,lrc->gr", past, masked[:step], preferred_element_type=jnp.float32
            )
        fresh = drive + jnp.dot(drive, correction.T, precision=lax.Precision.HIGHEST)
        results.append(fresh)
        if step < LATE:
            newest = gathered(fresh, 1)
            fresh_b.append(newest.astype(jnp.bfloat16))
    first = lax.axis_index("lag") == 0
    return lax.psum(jnp.where(first, jnp.stack(results, 0), 0.0), "lag")


def dot_rows(lhs, rhs):
    return lax.dot_general(lhs, rhs, (((1,), (1,)), ((), ())), preferred_element_type=jnp.float32)


def words_of(value, count):
    out = []
    for _ in range(count):
        word = value.astype(jnp.bfloat16)
        out.append(word)
        value = value - word.astype(jnp.float32)
    return out


def fetched(copies, sems):
    started = [
        pltpu.make_async_copy(source, target, sems.at[index])
        for index, (source, target) in enumerate(copies)
    ]
    for copy in started:
        copy.start()
    for copy in started:
        copy.wait()


def pack(history_in, neighbours_in, edge_coef_in, message, history, neighbours, edge_coef, sems):
    fetched(
        [(history_in, history), (neighbours_in, neighbours), (edge_coef_in, edge_coef)], sems
    )
    lags, gusts, rows = history.shape
    total = rows * lax.axis_size("elem")
    places = lax.axis_index("elem") * rows + lax.broadcasted_iota(
        jnp.int32, neighbours.shape, 1
    )
    offsets = lax.rem(neighbours[...] - places + (RIM + total), total)
    pieces = [history[lag] for lag in range(lags)]
    _, mid, low = words_of(history[0], 3)
    pieces += [mid.astype(jnp.float32), low.astype(jnp.float32), offsets.astype(jnp.float32)]
    pieces += [word.astype(jnp.float32) for word in words_of(edge_coef[...], 3)]
    pieces += [jnp.zeros_like(pieces[0])] * (message.shape[0] // gusts - len(pieces))
    message[...] = jnp.concatenate(pieces, axis=0).astype(jnp.bfloat16)


def live_piece(interaction, mask, lag, block, columns, lines):
    piece = interaction[lag, lines, columns]
    return jnp.where(mask[0, block, lag] != 0, piece, jnp.zeros_like(piece))


def make_near_load(
    mask_in, interaction_in, correction_in, own_c, near_load, mask, interaction, correction, sems
):
    fetched(
        [
            (mask_in, mask),
            (interaction_in.at[pl.ds(0, LATE)], interaction),
            (correction_in, correction),
        ],
        sems,
    )
    _, rows, total = interaction.shape
    cut = rows // 2
    own_c[...] = jnp.concatenate(words_of(correction[...], 2), axis=1)
    start = pl.multiple_of(lax.axis_index("gust") * cut, cut)
    places = [lag * total for lag in range(LATE - 1)] + [(LATE - 1) * total + 2 * rows]
    for lag, at in enumerate(places):
        for block in range(total // rows):
            near_load[:, pl.ds(at + block * rows, rows)] = live_piece(
                interaction, mask, lag, block, pl.ds(block * rows, rows), pl.ds(start, cut)
            )
    near_load[:, pl.ds((LATE - 1) * total, 2 * rows)] = own_c[pl.ds(start, cut), :]


def make_masked(mask_in, interaction, near_load, masked, mid_load, mask, sems):
    fetched([(mask_in, mask)], sems)
    lags, rows, total = interaction.shape
    for lag in range(lags):
        for block in range(total // rows):
            columns = pl.ds(block * rows, rows)
            masked[lag, :, columns] = live_piece(
                interaction, mask, lag, block, columns, pl.ds(0, rows)
            )
    mid_load[...] = near_load[:, : mid_load.shape[1]]


def relay(after, near, load):
    del after
    load[...] = near[:, : load.shape[1]]


def all_spread(after, everyone, spread):
    del after
    gusts = 4
    known = everyone.shape[0] // 2

    def piece(index):
        at = known + index * gusts
        return everyone[at : at + gusts, :].astype(jnp.float32)

    offsets = piece(2)
    coef = piece(3) + (piece(4) + piece(5))
    for d in range(2 * RIM):
        value = d if d < RIM else d + 1
        spread[d : d + 1, :] = jnp.sum(
            jnp.where(offsets == float(value), coef, 0.0), axis=0, keepdims=True
        )


def order(piece_0, piece_2, piece_3, piece_1, everyone, late):
    place = lax.axis_index("elem")
    rows = piece_0.shape[1]
    for flip, piece in enumerate((piece_0, piece_1, piece_2, piece_3)):
        start = pl.multiple_of((place ^ flip) * rows, rows)
        everyone[:, pl.ds(start, rows)] = piece[...]
    late[...] = everyone[late.shape[0] : 2 * late.shape[0], :]


def slope_of(newest, spread_ref):
    total = newest.shape[1]
    out = jnp.zeros_like(newest)
    for d in range(2 * RIM):
        shift = d - RIM if d < RIM else d - RIM + 1
        moved = pltpu.roll(newest, (-shift) % total, 1)
        out += spread_ref[d : d + 1, :] * (moved - newest)
    return out


def main_part(everyone, masked, part, slope, longer, spread, slopes):
    lags, rows, total = masked.shape
    gusts = 4
    known = lags * gusts
    wide = everyone[...].astype(jnp.float32)
    longer[...] = jnp.zeros_like(longer)
    longer[LATE * gusts : LATE * gusts + known, :] = wide[:known]
    acc = jnp.zeros(part.shape, jnp.float32)
    for lag in range(lags):
        lhs = longer[lag * gusts : lag * gusts + part.shape[0], :].astype(jnp.bfloat16)
        acc += dot_rows(lhs, masked[lag])
    part[...] = acc

    def piece(index):
        return wide[known + index * gusts : known + (index + 1) * gusts]

    newest = wide[:gusts] + (piece(0) + piece(1))
    offsets = piece(2)
    coef = piece(3) + (piece(4) + piece(5))
    for d in range(2 * RIM):
        value = d if d < RIM else d + 1
        spread[d : d + 1, :] = jnp.sum(
            jnp.where(offsets == float(value), coef, 0.0), axis=0, keepdims=True
        )
    newest = jnp.concatenate([newest, jnp.zeros_like(newest)], axis=0)
    slopes[...] = slope_of(newest, spread)
    start = pl.multiple_of(lax.axis_index("elem") * rows, rows)
    slope[...] = slopes[:, pl.ds(start, rows)]


def late_part(late, masked, part, both, longer):
    gusts = late.shape[0] // LATE
    value = late[...].astype(jnp.float32)
    longer[...] = jnp.zeros_like(longer)
    longer[: late.shape[0], :] = jnp.where(lax.axis_index("lag") == 0, 0.0, value)
    acc = part[...]
    for lag in range(LATE):
        lhs = longer[lag * gusts : lag * gusts + part.shape[0], :].astype(jnp.bfloat16)
        acc += dot_rows(lhs, masked[lag])
    both[...] = acc


def known_base(part, forcing, slope, ahead):
    gusts = forcing.shape[1]
    for step in range(STEPS):
        at = (STEPS - 1 - step) * gusts
        value = forcing[step] - part[at : at + gusts, :]
        if step == 0:
            value = value + slope[:gusts, :]
        ahead[step] = jnp.concatenate([value, jnp.zeros_like(value)], axis=0)


def make_base(after, ahead, other, base):
    del after
    gusts = 4
    for step in range(STEPS):
        at = (STEPS - 1 - step) * gusts
        value = other[at : at + gusts, :]
        base[step] = ahead[step] - jnp.concatenate([value, jnp.zeros_like(value)], axis=0)


def march(
    masked, load_1, load_2, load_3, swap_1, swap_2, swap_3, own_c,
    base_0, base_1, base_2, base_3, spread, out, near_out,
):
    place = lax.axis_index("elem")
    second = lax.axis_index("gust") == 1
    _, rows, total = masked.shape
    cut = rows // 2
    flips_of = range(total // rows)
    loads = (None, load_1, load_2, load_3)
    swaps = (None, swap_1, swap_2, swap_3)

    def flipped(values):
        odd = place % 2 == 1
        high = place // 2 == 1
        near = [jnp.where(odd, values[i ^ 1], values[i]) for i in flips_of]
        return [jnp.where(high, near[i ^ 2], near[i]) for i in flips_of]

    def rows_right(value):
        return jnp.where(second, pltpu.roll(value, cut, 1), value)

    def received(flip, start, count):
        columns = pl.ds(start, count)
        return jnp.concatenate([loads[flip][:, columns], swaps[flip][:, columns]], axis=0)

    def times(fresh_b, lag, flip):
        if flip == 0:
            return dot_rows(fresh_b, masked[lag])
        at = lag * total + (2 * rows if lag == LATE - 1 else 0)
        return rows_right(dot_rows(fresh_b, received(flip, at, total)))

    def corrected(drive, flip):
        lhs = jnp.concatenate(words_of(drive, 2), axis=0)
        added = 0.0
        for word in range(2):
            if flip == 0:
                rhs = own_c[:, word * rows : (word + 1) * rows]
            else:
                rhs = received(flip, (LATE - 1) * total + word * rows, rows)
            both = dot_rows(lhs, rhs)
            added = added + (both[:GUST_ROWS] + both[GUST_ROWS:])
        return drive + (added if flip == 0 else rows_right(added))

    marching = ((place == 1) | (place == 2)) & (lax.axis_index("lag") == 0)

    @pl.when(jnp.logical_not(marching))
    def _():
        out[...] = jnp.zeros_like(out)
        near_out[...] = jnp.zeros_like(near_out)

    @pl.when(marching)
    def _():
        waiting = [[base[step] for base in (base_0, base_1, base_2, base_3)] for step in range(STEPS)]
        waiting[LATE] = waiting[LATE][:2]
        for step in range(LATE):
            fresh = [corrected(waiting[step][flip], flip) for flip in flips_of]
            out[step], near_out[step] = fresh[:2]
            whole = jnp.concatenate(flipped(fresh), axis=1)
            fresh_b = whole.astype(jnp.bfloat16)
            slope = slope_of(whole, spread)
            slope = flipped([slope[:, i * rows : (i + 1) * rows] for i in flips_of])
            for later in range(step + 1, STEPS):
                lag = later - step - 1
                for flip in range(len(waiting[later])):
                    change = times(fresh_b, lag, flip)
                    if lag == 0:
                        change = change - slope[flip]
                    waiting[later][flip] = waiting[later][flip] - change
        out[LATE], near_out[LATE] = (corrected(waiting[LATE][flip], flip) for flip in (0, 1))


def on_core(body, shapes, operands, scratch=(), in_specs=None, limit=24, name=None, force=False):
    vmem = pl.BlockSpec(memory_space=pltpu.VMEM)
    return pl.pallas_call(
        body,
        out_shape=[
            pltpu.VMEM(shape, dtype) if force else jax.ShapeDtypeStruct(shape, dtype)
            for shape, dtype in shapes
        ],
        in_specs=in_specs or [vmem] * len(operands),
        out_specs=[vmem] * len(shapes),
        scratch_shapes=list(scratch),
        cost_estimate=pl.CostEstimate(flops=10**10, bytes_accessed=2**20, transcendentals=0),
        compiler_params=pltpu.CompilerParams(vmem_limit_bytes=limit * 2**20 if limit else None),
        name=name,
    )(*operands)


def exchanged(value, pairs, count):
    named = {source for source, _ in pairs}
    moves = [(2 * a + core, 2 * b + core) for a, b in pairs for core in (0, 1)]
    moves += [
        (2 * i + core, 2 * i + 1 - core) for i in range(count) if i not in named for core in (0, 1)
    ]
    return lax.ppermute(value, ("elem", "lag", "gust"), moves)


def places_march(history, forcing, interaction, block_mask, correction, neighbours, edge_coef):
    f32, bf16 = jnp.float32, jnp.bfloat16
    rows = correction.shape[0]
    lags, gusts, _ = history.shape
    count = lax.axis_size("elem")
    total = rows * count
    part_rows = 24
    width = (LATE - 1) * total + 2 * rows
    anywhere = pl.BlockSpec(memory_space=pl.ANY)
    vmem = pl.BlockSpec(memory_space=pltpu.VMEM)

    def like(value):
        return pltpu.VMEM(value.shape, value.dtype)

    def crossed(value, axis):
        return lax.ppermute(value, axis, [(0, 1), (1, 0)])

    (message,) = on_core(
        pack,
        [((64, rows), bf16)],
        (history, neighbours, edge_coef),
        scratch=[like(history), like(neighbours), like(edge_coef), pltpu.SemaphoreType.DMA((3,))],
        in_specs=[anywhere] * 3,
        limit=None,
        force=True,
        name="pack",
    )
    messages = flips(message)
    mask = jnp.transpose(block_mask, (1, 2, 0))
    after_message, _ = lax.optimization_barrier((correction, message))
    own_c, near_load = on_core(
        make_near_load,
        [((rows, 2 * rows), bf16), ((rows // 2, width + total), bf16)],
        (mask, interaction, after_message),
        scratch=[
            pltpu.SMEM(mask.shape, mask.dtype),
            pltpu.VMEM((LATE, rows, total), bf16),
            like(correction),
            pltpu.SemaphoreType.DMA((3,)),
        ],
        in_specs=[anywhere] * 3,
        name="near_load",
    )
    masked, mid_load = on_core(
        make_masked,
        [(interaction.shape, bf16), ((rows // 2, width), bf16)],
        (mask, interaction, near_load),
        scratch=[pltpu.SMEM(mask.shape, mask.dtype), pltpu.SemaphoreType.DMA((1,))],
        in_specs=[anywhere, vmem, vmem],
        name="masked",
    )
    everyone, late = on_core(
        order,
        [((64, total), bf16), ((LATE * gusts, total), bf16)],
        [messages[flip] for flip in (0, 2, 3, 1)],
        name="order",
    )
    before = crossed(late, "lag")
    part, slope = on_core(
        main_part,
        [((part_rows, rows), f32), ((GUST_ROWS, rows), f32)],
        (everyone, masked),
        scratch=[
            pltpu.VMEM((56, total), f32),
            pltpu.VMEM((2 * RIM, total), f32),
            pltpu.VMEM((GUST_ROWS, total), f32),
        ],
        name="main_part",
    )

    mid_load, _ = lax.optimization_barrier((mid_load, own_c))

    def bulk(value, pairs):
        return exchanged(value, [(2 * a, 2 * b) for a, b in pairs], 2 * count)

    near = bulk(near_load, NEAR)
    mid = bulk(mid_load, MID)

    (part,) = on_core(
        late_part,
        [((part_rows, rows), f32)],
        (before, masked, part),
        scratch=[pltpu.VMEM((40, total), f32)],
        name="late_part",
    )
    other = crossed(part, "lag")
    (ahead,) = on_core(
        known_base,
        [((STEPS, GUST_ROWS, rows), f32)],
        (part, forcing, slope),
        name="known_base",
    )
    (far_load,) = on_core(
        relay, [((rows // 2, width), bf16)], (ahead, near), in_specs=[anywhere, vmem], name="relay"
    )
    far = bulk(far_load, MID)
    early, _ = lax.optimization_barrier(((near, mid), ahead))
    near_swap, mid_swap = (crossed(piece, "gust") for piece in early)
    (base,) = on_core(
        make_base,
        [((STEPS, GUST_ROWS, rows), f32)],
        (far_load, ahead, other),
        in_specs=[anywhere, vmem, vmem],
        name="base",
    )
    bases = [base] + [bulk(base, pairs) for pairs in (NEAR, FAR, MID)]
    (spread,) = on_core(
        all_spread,
        [((2 * RIM, total), f32)],
        (base, everyone),
        in_specs=[anywhere, vmem],
        name="spread",
    )
    far, _ = lax.optimization_barrier((far, bases[3]))
    far_swap = crossed(far, "gust")
    own, outer = on_core(
        march,
        [((STEPS, GUST_ROWS, rows), f32)] * 2,
        (masked, near, far, mid, near_swap, far_swap, mid_swap, own_c, *bases, spread),
        name="march",
    )

    def handed(value, *cycles):
        moves = []
        for cycle in cycles:
            moves += zip(cycle, cycle[1:] + cycle[:1])
        return exchanged(value, moves, 2 * count)

    to_both = handed(outer, [2, 1, 3], [4, 7, 5])
    to_outer = handed(outer, [2, 0], [4, 6])
    to_lag = handed(own, [2, 3], [4, 5])
    place = lax.axis_index("elem")
    inside = (place == 1) | (place == 2)
    first = lax.axis_index("lag") == 0
    result = jnp.where(
        inside, jnp.where(first, own, to_lag), jnp.where(first, to_outer, to_both)
    )
    return result[:, :gusts]


def solution(mesh):
    placed = (
        P("lag", ("groups", "gust"), "elem"),
        P(None, ("groups", "gust"), "elem"),
        P("lag", "elem", None),
        P("lag", "elem", None),
        P("elem", None),
        P(None, "elem"),
        P(None, "elem"),
    )
    small = mesh.shape["elem"] == 4 and mesh.shape["lag"] == 2 and mesh.shape["gust"] == 2
    return jax.shard_map(
        places_march if small else exchange_each_step,
        mesh=mesh,
        in_specs=placed,
        out_specs=P(None, ("groups", "gust"), "elem"),
        check_vma=False,
    )
```

```python
import jax
import jax.numpy as jnp
from jax import lax
from jax.experimental import pallas as pl
from jax.experimental.pallas import tpu as pltpu
from jax.sharding import PartitionSpec as P

RIM = 8
STEPS = 5
LATE = STEPS - 1
GUST_ROWS = 8
NEAR = ((0, 1), (1, 0), (2, 3), (3, 2))
MID = ((1, 2), (2, 1))
FAR = ((0, 2), (2, 0), (1, 3), (3, 1))


def flips(value, flipped=(1, 2, 3)):
    count = lax.axis_size("elem")
    return [value] + [
        lax.ppermute(value, "elem", [(i, i ^ flip) for i in range(count)]) for flip in flipped
    ]


def lag_behind(value):
    count = lax.axis_size("lag")
    moved = lax.ppermute(value, "lag", [(i, (i + 1) % count) for i in range(count)])
    return jnp.where(lax.axis_index("lag") == 0, jnp.zeros_like(moved), moved)


def by_offset(neighbours, edge_coef):
    rows = neighbours.shape[1]
    total = rows * lax.axis_size("elem")
    places = lax.axis_index("elem") * rows + jnp.arange(rows, dtype=jnp.int32)
    return (neighbours - places[None, :] + RIM) % total


def spread_weights(offsets, edge_coef):
    return [
        jnp.sum(jnp.where(offsets == d, edge_coef, 0.0), axis=0, keepdims=True)
        for d in range(2 * RIM + 1)
    ]


def own_gradient(newest, spread):
    rows = spread[0].shape[1]
    total = newest.shape[1]
    wide = jnp.concatenate([newest[:, total - RIM :], newest, newest[:, :RIM]], axis=1)
    start = lax.axis_index("elem") * rows
    window = lax.dynamic_slice(wide, (0, start), (newest.shape[0], rows + 2 * RIM))
    own = window[:, RIM : RIM + rows]
    out = jnp.zeros_like(own)
    for d in range(2 * RIM + 1):
        if d != RIM:
            out += spread[d] * (window[:, d : d + rows] - own)
    return out


def known_part(hist, masked):
    lags, gusts, total = hist.shape
    longer = jnp.concatenate([lag_behind(hist[lags - LATE :]), hist], axis=0)
    stacked = jnp.stack(
        [longer[LATE - step : LATE - step + lags] for step in range(STEPS)], axis=1
    ).reshape(lags, STEPS * gusts, total)
    part = jnp.einsum("lmc,lrc->mr", stacked, masked, preferred_element_type=jnp.float32)
    return part.reshape(STEPS, gusts, masked.shape[1])


def live_coefficients(interaction, block_mask, rows):
    live = jnp.repeat(block_mask[:, 0, :].astype(jnp.bfloat16), rows, axis=1)
    return interaction * live[:, None, :]


def exchange_each_step(
    history, forcing, interaction, block_mask, correction, neighbours, edge_coef
):
    rows = correction.shape[0]
    masked = live_coefficients(interaction, block_mask, rows)
    spread = spread_weights(by_offset(neighbours, edge_coef), edge_coef)

    def gathered(value, dim):
        return lax.all_gather(value, "elem", axis=dim, tiled=True)

    hist = gathered(history.astype(jnp.bfloat16), 2)
    newest = gathered(history[0], 1)
    base = forcing - lax.psum(known_part(hist, masked), "lag")
    fresh_b = []
    results = []
    for step in range(STEPS):
        drive = base[step] + own_gradient(newest, spread)
        if step:
            past = jnp.stack(fresh_b[::-1], axis=0)
            drive -= jnp.einsum(
                "lgc,lrc->gr", past, masked[:step], preferred_element_type=jnp.float32
            )
        fresh = drive + jnp.dot(drive, correction.T, precision=lax.Precision.HIGHEST)
        results.append(fresh)
        if step < LATE:
            newest = gathered(fresh, 1)
            fresh_b.append(newest.astype(jnp.bfloat16))
    first = lax.axis_index("lag") == 0
    return lax.psum(jnp.where(first, jnp.stack(results, 0), 0.0), "lag")


def dot_rows(lhs, rhs):
    return lax.dot_general(lhs, rhs, (((1,), (1,)), ((), ())), preferred_element_type=jnp.float32)


def words_of(value, count):
    out = []
    for _ in range(count):
        word = value.astype(jnp.bfloat16)
        out.append(word)
        value = value - word.astype(jnp.float32)
    return out


def fetched(copies, sems):
    started = [
        pltpu.make_async_copy(source, target, sems.at[index])
        for index, (source, target) in enumerate(copies)
    ]
    for copy in started:
        copy.start()
    for copy in started:
        copy.wait()


def pack(history_in, neighbours_in, edge_coef_in, message, history, neighbours, edge_coef, sems):
    fetched(
        [(history_in, history), (neighbours_in, neighbours), (edge_coef_in, edge_coef)], sems
    )
    lags, gusts, rows = history.shape
    total = rows * lax.axis_size("elem")
    places = lax.axis_index("elem") * rows + lax.broadcasted_iota(
        jnp.int32, neighbours.shape, 1
    )
    offsets = lax.rem(neighbours[...] - places + (RIM + total), total)
    pieces = [history[lag] for lag in range(lags)]
    _, mid, low = words_of(history[0], 3)
    pieces += [mid.astype(jnp.float32), low.astype(jnp.float32), offsets.astype(jnp.float32)]
    pieces += [word.astype(jnp.float32) for word in words_of(edge_coef[...], 3)]
    pieces += [jnp.zeros_like(pieces[0])] * (message.shape[0] // gusts - len(pieces))
    message[...] = jnp.concatenate(pieces, axis=0).astype(jnp.bfloat16)


def live_piece(interaction, mask, lag, block, columns, lines):
    piece = interaction[lag, lines, columns]
    return jnp.where(mask[0, block, lag] != 0, piece, jnp.zeros_like(piece))


def make_near_load(
    mask_in, interaction_in, correction_in, own_c, near_load, mask, interaction, correction, sems
):
    fetched(
        [
            (mask_in, mask),
            (interaction_in.at[pl.ds(0, LATE)], interaction),
            (correction_in, correction),
        ],
        sems,
    )
    _, rows, total = interaction.shape
    cut = rows // 2
    own_c[...] = jnp.concatenate(words_of(correction[...], 2), axis=1)
    start = pl.multiple_of(lax.axis_index("gust") * cut, cut)
    places = [lag * total for lag in range(LATE - 1)] + [(LATE - 1) * total + 2 * rows]
    for lag, at in enumerate(places):
        for block in range(total // rows):
            near_load[:, pl.ds(at + block * rows, rows)] = live_piece(
                interaction, mask, lag, block, pl.ds(block * rows, rows), pl.ds(start, cut)
            )
    near_load[:, pl.ds((LATE - 1) * total, 2 * rows)] = own_c[pl.ds(start, cut), :]


def make_masked(mask_in, interaction, near_load, masked, mid_load, mask, sems):
    fetched([(mask_in, mask)], sems)
    lags, rows, total = interaction.shape
    for lag in range(lags):
        for block in range(total // rows):
            columns = pl.ds(block * rows, rows)
            masked[lag, :, columns] = live_piece(
                interaction, mask, lag, block, columns, pl.ds(0, rows)
            )
    mid_load[...] = near_load[:, : mid_load.shape[1]]


def relay(after, near, load):
    del after
    load[...] = near[:, : load.shape[1]]


def all_spread(after, everyone, spread):
    del after
    gusts = 4
    known = everyone.shape[0] // 2

    def piece(index):
        at = known + index * gusts
        return everyone[at : at + gusts, :].astype(jnp.float32)

    offsets = piece(2)
    coef = piece(3) + (piece(4) + piece(5))
    for d in range(2 * RIM):
        value = d if d < RIM else d + 1
        spread[d : d + 1, :] = jnp.sum(
            jnp.where(offsets == float(value), coef, 0.0), axis=0, keepdims=True
        )


def order(piece_0, piece_2, piece_3, piece_1, everyone, late):
    place = lax.axis_index("elem")
    rows = piece_0.shape[1]
    for flip, piece in enumerate((piece_0, piece_1, piece_2, piece_3)):
        start = pl.multiple_of((place ^ flip) * rows, rows)
        everyone[:, pl.ds(start, rows)] = piece[...]
    late[...] = everyone[late.shape[0] : 2 * late.shape[0], :]


def slope_of(newest, spread_ref):
    total = newest.shape[1]
    out = jnp.zeros_like(newest)
    for d in range(2 * RIM):
        shift = d - RIM if d < RIM else d - RIM + 1
        moved = pltpu.roll(newest, (-shift) % total, 1)
        out += spread_ref[d : d + 1, :] * (moved - newest)
    return out


def main_part(everyone, masked, part, slope, longer, spread, slopes):
    lags, rows, total = masked.shape
    gusts = 4
    known = lags * gusts
    wide = everyone[...].astype(jnp.float32)
    longer[...] = jnp.zeros_like(longer)
    longer[LATE * gusts : LATE * gusts + known, :] = wide[:known]
    acc = jnp.zeros(part.shape, jnp.float32)
    for lag in range(lags):
        lhs = longer[lag * gusts : lag * gusts + part.shape[0], :].astype(jnp.bfloat16)
        acc += dot_rows(lhs, masked[lag])
    part[...] = acc

    def piece(index):
        return wide[known + index * gusts : known + (index + 1) * gusts]

    newest = wide[:gusts] + (piece(0) + piece(1))
    offsets = piece(2)
    coef = piece(3) + (piece(4) + piece(5))
    for d in range(2 * RIM):
        value = d if d < RIM else d + 1
        spread[d : d + 1, :] = jnp.sum(
            jnp.where(offsets == float(value), coef, 0.0), axis=0, keepdims=True
        )
    newest = jnp.concatenate([newest, jnp.zeros_like(newest)], axis=0)
    slopes[...] = slope_of(newest, spread)
    start = pl.multiple_of(lax.axis_index("elem") * rows, rows)
    slope[...] = slopes[:, pl.ds(start, rows)]


def late_part(late, masked, part, both, longer):
    gusts = late.shape[0] // LATE
    first = lax.axis_index("lag") == 0

    @pl.when(first)
    def _():
        both[...] = part[...]

    @pl.when(jnp.logical_not(first))
    def _():
        longer[...] = jnp.zeros_like(longer)
        longer[: late.shape[0], :] = late[...].astype(jnp.float32)
        acc = part[...]
        for lag in range(LATE):
            lhs = longer[lag * gusts : lag * gusts + part.shape[0], :].astype(jnp.bfloat16)
            acc += dot_rows(lhs, masked[lag])
        both[...] = acc


def known_base(part, forcing, slope, ahead):
    gusts = forcing.shape[1]
    values = []
    for step in range(STEPS):
        at = (STEPS - 1 - step) * gusts
        value = forcing[step] - part[at : at + gusts, :]
        if step == 0:
            value = value + slope[:gusts, :]
        values.append(value)
    values.append(jnp.zeros_like(values[0]))
    ahead[...] = jnp.concatenate(values, axis=0)


def make_base(after, ahead, other, base):
    del after
    gusts = 4
    values = [other[at * gusts : (at + 1) * gusts, :] for at in reversed(range(STEPS))]
    values.append(jnp.zeros_like(values[0]))
    base[...] = ahead[...] - jnp.concatenate(values, axis=0)


def march(
    masked, load_1, load_2, load_3, swap_1, swap_2, swap_3, own_c,
    base_0, base_1, base_2, base_3, spread, out, near_out,
):
    place = lax.axis_index("elem")
    second = lax.axis_index("gust") == 1
    _, rows, total = masked.shape
    cut = rows // 2
    flips_of = range(total // rows)
    loads = (None, load_1, load_2, load_3)
    swaps = (None, swap_1, swap_2, swap_3)

    def flipped(values):
        odd = place % 2 == 1
        high = place // 2 == 1
        near = [jnp.where(odd, values[i ^ 1], values[i]) for i in flips_of]
        return [jnp.where(high, near[i ^ 2], near[i]) for i in flips_of]

    def rows_right(value):
        return jnp.where(second, pltpu.roll(value, cut, 1), value)

    def received(flip, start, count):
        columns = pl.ds(start, count)
        return jnp.concatenate([loads[flip][:, columns], swaps[flip][:, columns]], axis=0)

    def times(fresh_b, lag, flip):
        if flip == 0:
            return dot_rows(fresh_b, masked[lag])
        at = lag * total + (2 * rows if lag == LATE - 1 else 0)
        return rows_right(dot_rows(fresh_b, received(flip, at, total)))

    def corrected(drive, flip):
        lhs = jnp.concatenate(words_of(drive, 2), axis=0)
        added = 0.0
        for word in range(2):
            if flip == 0:
                rhs = own_c[:, word * rows : (word + 1) * rows]
            else:
                rhs = received(flip, (LATE - 1) * total + word * rows, rows)
            both = dot_rows(lhs, rhs)
            added = added + (both[:GUST_ROWS] + both[GUST_ROWS:])
        return drive + (added if flip == 0 else rows_right(added))

    marching = ((place == 1) | (place == 2)) & (lax.axis_index("lag") == 0)

    @pl.when(jnp.logical_not(marching))
    def _():
        out[...] = jnp.zeros_like(out)
        near_out[...] = jnp.zeros_like(near_out)

    @pl.when(marching)
    def _():
        waiting = [
            [base[step * 4 : step * 4 + GUST_ROWS, :] for base in (base_0, base_1, base_2, base_3)]
            for step in range(STEPS)
        ]
        waiting[LATE] = waiting[LATE][:2]
        for step in range(LATE):
            fresh = [corrected(waiting[step][flip], flip) for flip in flips_of]
            out[step], near_out[step] = fresh[:2]
            whole = jnp.concatenate(flipped(fresh), axis=1)
            fresh_b = whole.astype(jnp.bfloat16)
            slope = slope_of(whole, spread)
            slope = flipped([slope[:, i * rows : (i + 1) * rows] for i in flips_of])
            for later in range(step + 1, STEPS):
                lag = later - step - 1
                for flip in range(len(waiting[later])):
                    change = times(fresh_b, lag, flip)
                    if lag == 0:
                        change = change - slope[flip]
                    waiting[later][flip] = waiting[later][flip] - change
        out[LATE], near_out[LATE] = (corrected(waiting[LATE][flip], flip) for flip in (0, 1))


def on_core(body, shapes, operands, scratch=(), in_specs=None, limit=24, name=None, force=False):
    vmem = pl.BlockSpec(memory_space=pltpu.VMEM)
    return pl.pallas_call(
        body,
        out_shape=[
            pltpu.VMEM(shape, dtype) if force else jax.ShapeDtypeStruct(shape, dtype)
            for shape, dtype in shapes
        ],
        in_specs=in_specs or [vmem] * len(operands),
        out_specs=[vmem] * len(shapes),
        scratch_shapes=list(scratch),
        cost_estimate=pl.CostEstimate(flops=10**10, bytes_accessed=2**20, transcendentals=0),
        compiler_params=pltpu.CompilerParams(vmem_limit_bytes=limit * 2**20 if limit else None),
        name=name,
    )(*operands)


def exchanged(value, pairs, count):
    named = {source for source, _ in pairs}
    moves = [(2 * a + core, 2 * b + core) for a, b in pairs for core in (0, 1)]
    moves += [
        (2 * i + core, 2 * i + 1 - core) for i in range(count) if i not in named for core in (0, 1)
    ]
    return lax.ppermute(value, ("elem", "lag", "gust"), moves)


def places_march(history, forcing, interaction, block_mask, correction, neighbours, edge_coef):
    f32, bf16 = jnp.float32, jnp.bfloat16
    rows = correction.shape[0]
    lags, gusts, _ = history.shape
    count = lax.axis_size("elem")
    total = rows * count
    part_rows = 24
    width = (LATE - 1) * total + 2 * rows
    anywhere = pl.BlockSpec(memory_space=pl.ANY)
    vmem = pl.BlockSpec(memory_space=pltpu.VMEM)

    def like(value):
        return pltpu.VMEM(value.shape, value.dtype)

    def crossed(value, axis):
        return lax.ppermute(value, axis, [(0, 1), (1, 0)])

    (message,) = on_core(
        pack,
        [((64, rows), bf16)],
        (history, neighbours, edge_coef),
        scratch=[like(history), like(neighbours), like(edge_coef), pltpu.SemaphoreType.DMA((3,))],
        in_specs=[anywhere] * 3,
        limit=None,
        force=True,
        name="pack",
    )
    messages = flips(message)
    mask = jnp.transpose(block_mask, (1, 2, 0))
    after_message, _ = lax.optimization_barrier((correction, message))
    own_c, near_load = on_core(
        make_near_load,
        [((rows, 2 * rows), bf16), ((rows // 2, width + total), bf16)],
        (mask, interaction, after_message),
        scratch=[
            pltpu.SMEM(mask.shape, mask.dtype),
            pltpu.VMEM((LATE, rows, total), bf16),
            like(correction),
            pltpu.SemaphoreType.DMA((3,)),
        ],
        in_specs=[anywhere] * 3,
        name="near_load",
    )
    masked, mid_load = on_core(
        make_masked,
        [(interaction.shape, bf16), ((rows // 2, width), bf16)],
        (mask, interaction, near_load),
        scratch=[pltpu.SMEM(mask.shape, mask.dtype), pltpu.SemaphoreType.DMA((1,))],
        in_specs=[anywhere, vmem, vmem],
        name="masked",
    )
    everyone, late = on_core(
        order,
        [((64, total), bf16), ((LATE * gusts, total), bf16)],
        [messages[flip] for flip in (0, 2, 3, 1)],
        name="order",
    )
    before = crossed(late, "lag")
    part, slope = on_core(
        main_part,
        [((part_rows, rows), f32), ((GUST_ROWS, rows), f32)],
        (everyone, masked),
        scratch=[
            pltpu.VMEM((56, total), f32),
            pltpu.VMEM((2 * RIM, total), f32),
            pltpu.VMEM((GUST_ROWS, total), f32),
        ],
        name="main_part",
    )

    mid_load, _ = lax.optimization_barrier((mid_load, own_c))

    def bulk(value, pairs):
        return exchanged(value, [(2 * a, 2 * b) for a, b in pairs], 2 * count)

    near = bulk(near_load, NEAR)
    mid = bulk(mid_load, MID)

    (part,) = on_core(
        late_part,
        [((part_rows, rows), f32)],
        (before, masked, part),
        scratch=[pltpu.VMEM((40, total), f32)],
        name="late_part",
    )
    other = crossed(part, "lag")
    (ahead,) = on_core(
        known_base,
        [((part_rows, rows), f32)],
        (part, forcing, slope),
        name="known_base",
    )
    (far_load,) = on_core(
        relay, [((rows // 2, width), bf16)], (ahead, near), in_specs=[anywhere, vmem], name="relay"
    )
    far = bulk(far_load, MID)
    early, _ = lax.optimization_barrier(((near, mid), ahead))
    near_swap, mid_swap = (crossed(piece, "gust") for piece in early)
    (base,) = on_core(
        make_base,
        [((part_rows, rows), f32)],
        (far_load, ahead, other),
        in_specs=[anywhere, vmem, vmem],
        name="base",
    )
    bases = [base] + [bulk(base, pairs) for pairs in (NEAR, FAR, MID)]
    (spread,) = on_core(
        all_spread,
        [((2 * RIM, total), f32)],
        (base, everyone),
        in_specs=[anywhere, vmem],
        name="spread",
    )
    far, _ = lax.optimization_barrier((far, bases[3]))
    far_swap = crossed(far, "gust")
    own, outer = on_core(
        march,
        [((STEPS, GUST_ROWS, rows), f32)] * 2,
        (masked, near, far, mid, near_swap, far_swap, mid_swap, own_c, *bases, spread),
        name="march",
    )

    def handed(value, *cycles):
        moves = []
        for cycle in cycles:
            moves += zip(cycle, cycle[1:] + cycle[:1])
        return exchanged(value, moves, 2 * count)

    to_both = handed(outer, [2, 1, 3], [4, 7, 5])
    to_outer = handed(outer, [2, 0], [4, 6])
    to_lag = handed(own, [2, 3], [4, 5])
    place = lax.axis_index("elem")
    inside = (place == 1) | (place == 2)
    first = lax.axis_index("lag") == 0
    result = jnp.where(
        inside, jnp.where(first, own, to_lag), jnp.where(first, to_outer, to_both)
    )
    return result[:, :gusts]


def solution(mesh):
    placed = (
        P("lag", ("groups", "gust"), "elem"),
        P(None, ("groups", "gust"), "elem"),
        P("lag", "elem", None),
        P("lag", "elem", None),
        P("elem", None),
        P(None, "elem"),
        P(None, "elem"),
    )
    small = mesh.shape["elem"] == 4 and mesh.shape["lag"] == 2 and mesh.shape["gust"] == 2
    return jax.shard_map(
        places_march if small else exchange_each_step,
        mesh=mesh,
        in_specs=placed,
        out_specs=P(None, ("groups", "gust"), "elem"),
        check_vma=False,
    )
```

```python
import jax
import jax.numpy as jnp
from jax import lax
from jax.experimental import pallas as pl
from jax.experimental.pallas import tpu as pltpu
from jax.sharding import PartitionSpec as P

RIM = 8
STEPS = 5
LATE = STEPS - 1
GUST_ROWS = 8
NEAR = ((0, 1), (1, 0), (2, 3), (3, 2))
MID = ((1, 2), (2, 1))
FAR = ((0, 2), (2, 0), (1, 3), (3, 1))


def flips(value, flipped=(1, 2, 3)):
    count = lax.axis_size("elem")
    return [value] + [
        lax.ppermute(value, "elem", [(i, i ^ flip) for i in range(count)]) for flip in flipped
    ]


def lag_behind(value):
    count = lax.axis_size("lag")
    moved = lax.ppermute(value, "lag", [(i, (i + 1) % count) for i in range(count)])
    return jnp.where(lax.axis_index("lag") == 0, jnp.zeros_like(moved), moved)


def by_offset(neighbours, edge_coef):
    rows = neighbours.shape[1]
    total = rows * lax.axis_size("elem")
    places = lax.axis_index("elem") * rows + jnp.arange(rows, dtype=jnp.int32)
    return (neighbours - places[None, :] + RIM) % total


def spread_weights(offsets, edge_coef):
    return [
        jnp.sum(jnp.where(offsets == d, edge_coef, 0.0), axis=0, keepdims=True)
        for d in range(2 * RIM + 1)
    ]


def own_gradient(newest, spread):
    rows = spread[0].shape[1]
    total = newest.shape[1]
    wide = jnp.concatenate([newest[:, total - RIM :], newest, newest[:, :RIM]], axis=1)
    start = lax.axis_index("elem") * rows
    window = lax.dynamic_slice(wide, (0, start), (newest.shape[0], rows + 2 * RIM))
    own = window[:, RIM : RIM + rows]
    out = jnp.zeros_like(own)
    for d in range(2 * RIM + 1):
        if d != RIM:
            out += spread[d] * (window[:, d : d + rows] - own)
    return out


def known_part(hist, masked):
    lags, gusts, total = hist.shape
    longer = jnp.concatenate([lag_behind(hist[lags - LATE :]), hist], axis=0)
    stacked = jnp.stack(
        [longer[LATE - step : LATE - step + lags] for step in range(STEPS)], axis=1
    ).reshape(lags, STEPS * gusts, total)
    part = jnp.einsum("lmc,lrc->mr", stacked, masked, preferred_element_type=jnp.float32)
    return part.reshape(STEPS, gusts, masked.shape[1])


def live_coefficients(interaction, block_mask, rows):
    live = jnp.repeat(block_mask[:, 0, :].astype(jnp.bfloat16), rows, axis=1)
    return interaction * live[:, None, :]


def exchange_each_step(
    history, forcing, interaction, block_mask, correction, neighbours, edge_coef
):
    rows = correction.shape[0]
    masked = live_coefficients(interaction, block_mask, rows)
    spread = spread_weights(by_offset(neighbours, edge_coef), edge_coef)

    def gathered(value, dim):
        return lax.all_gather(value, "elem", axis=dim, tiled=True)

    hist = gathered(history.astype(jnp.bfloat16), 2)
    newest = gathered(history[0], 1)
    base = forcing - lax.psum(known_part(hist, masked), "lag")
    fresh_b = []
    results = []
    for step in range(STEPS):
        drive = base[step] + own_gradient(newest, spread)
        if step:
            past = jnp.stack(fresh_b[::-1], axis=0)
            drive -= jnp.einsum(
                "lgc,lrc->gr", past, masked[:step], preferred_element_type=jnp.float32
            )
        fresh = drive + jnp.dot(drive, correction.T, precision=lax.Precision.HIGHEST)
        results.append(fresh)
        if step < LATE:
            newest = gathered(fresh, 1)
            fresh_b.append(newest.astype(jnp.bfloat16))
    first = lax.axis_index("lag") == 0
    return lax.psum(jnp.where(first, jnp.stack(results, 0), 0.0), "lag")


def dot_rows(lhs, rhs):
    return lax.dot_general(lhs, rhs, (((1,), (1,)), ((), ())), preferred_element_type=jnp.float32)


def words_of(value, count):
    out = []
    for _ in range(count):
        word = value.astype(jnp.bfloat16)
        out.append(word)
        value = value - word.astype(jnp.float32)
    return out


def fetched(copies, sems):
    started = [
        pltpu.make_async_copy(source, target, sems.at[index])
        for index, (source, target) in enumerate(copies)
    ]
    for copy in started:
        copy.start()
    for copy in started:
        copy.wait()


def pack(history_in, neighbours_in, edge_coef_in, message, history, neighbours, edge_coef, sems):
    fetched(
        [(history_in, history), (neighbours_in, neighbours), (edge_coef_in, edge_coef)], sems
    )
    lags, gusts, rows = history.shape
    total = rows * lax.axis_size("elem")
    places = lax.axis_index("elem") * rows + lax.broadcasted_iota(
        jnp.int32, neighbours.shape, 1
    )
    offsets = lax.rem(neighbours[...] - places + (RIM + total), total)
    pieces = [history[lag] for lag in range(lags)]
    _, mid, low = words_of(history[0], 3)
    pieces += [mid.astype(jnp.float32), low.astype(jnp.float32), offsets.astype(jnp.float32)]
    pieces += [word.astype(jnp.float32) for word in words_of(edge_coef[...], 3)]
    pieces += [jnp.zeros_like(pieces[0])] * (message.shape[0] // gusts - len(pieces))
    message[...] = jnp.concatenate(pieces, axis=0).astype(jnp.bfloat16)


def live_piece(interaction, mask, lag, block, columns, lines):
    piece = interaction[lag, lines, columns]
    return jnp.where(mask[0, block, lag] != 0, piece, jnp.zeros_like(piece))


def make_near_load(
    mask_in, interaction_in, correction_in, own_c, near_load, mask, interaction, correction, sems
):
    fetched(
        [
            (mask_in, mask),
            (interaction_in.at[pl.ds(0, LATE)], interaction),
            (correction_in, correction),
        ],
        sems,
    )
    _, rows, total = interaction.shape
    cut = rows // 2
    own_c[...] = jnp.concatenate(words_of(correction[...], 2), axis=1)
    start = pl.multiple_of(lax.axis_index("gust") * cut, cut)
    places = [lag * total for lag in range(LATE - 1)] + [(LATE - 1) * total + 2 * rows]
    for lag, at in enumerate(places):
        for block in range(total // rows):
            near_load[:, pl.ds(at + block * rows, rows)] = live_piece(
                interaction, mask, lag, block, pl.ds(block * rows, rows), pl.ds(start, cut)
            )
    near_load[:, pl.ds((LATE - 1) * total, 2 * rows)] = own_c[pl.ds(start, cut), :]


def make_masked(mask_in, interaction, near_load, masked, mid_load, mask, sems):
    fetched([(mask_in, mask)], sems)
    lags, rows, total = interaction.shape
    for lag in range(lags):
        for block in range(total // rows):
            columns = pl.ds(block * rows, rows)
            masked[lag, :, columns] = live_piece(
                interaction, mask, lag, block, columns, pl.ds(0, rows)
            )
    mid_load[...] = near_load[:, : mid_load.shape[1]]


def relay(after, near, load):
    del after
    load[...] = near[:, : load.shape[1]]


def all_spread(after, everyone, spread):
    del after
    gusts = 4
    known = everyone.shape[0] // 2
    extra = everyone[known : 2 * known, :].astype(jnp.float32)

    def piece(index):
        return extra[index * gusts : (index + 1) * gusts]

    offsets = piece(2)
    coef = piece(3) + (piece(4) + piece(5))
    for d in range(2 * RIM):
        value = d if d < RIM else d + 1
        spread[d : d + 1, :] = jnp.sum(
            jnp.where(offsets == float(value), coef, 0.0), axis=0, keepdims=True
        )


def order(piece_0, piece_2, piece_3, piece_1, everyone, late):
    place = lax.axis_index("elem")
    rows = piece_0.shape[1]
    for flip, piece in enumerate((piece_0, piece_1, piece_2, piece_3)):
        start = pl.multiple_of((place ^ flip) * rows, rows)
        everyone[:, pl.ds(start, rows)] = piece[...]
    late[...] = everyone[late.shape[0] : 2 * late.shape[0], :]


def slope_of(newest, spread_ref):
    total = newest.shape[1]
    out = jnp.zeros_like(newest)
    for d in range(2 * RIM):
        shift = d - RIM if d < RIM else d - RIM + 1
        moved = pltpu.roll(newest, (-shift) % total, 1)
        out += spread_ref[d : d + 1, :] * (moved - newest)
    return out


def main_part(everyone, masked, part, slope, longer, spread, slopes):
    lags, rows, total = masked.shape
    gusts = 4
    known = lags * gusts
    wide = everyone[...].astype(jnp.float32)
    longer[...] = jnp.zeros_like(longer)
    longer[LATE * gusts : LATE * gusts + known, :] = wide[:known]
    acc = jnp.zeros(part.shape, jnp.float32)
    for lag in range(lags):
        lhs = longer[lag * gusts : lag * gusts + part.shape[0], :].astype(jnp.bfloat16)
        acc += dot_rows(lhs, masked[lag])
    part[...] = acc

    def piece(index):
        return wide[known + index * gusts : known + (index + 1) * gusts]

    newest = wide[:gusts] + (piece(0) + piece(1))
    offsets = piece(2)
    coef = piece(3) + (piece(4) + piece(5))
    for d in range(2 * RIM):
        value = d if d < RIM else d + 1
        spread[d : d + 1, :] = jnp.sum(
            jnp.where(offsets == float(value), coef, 0.0), axis=0, keepdims=True
        )
    newest = jnp.concatenate([newest, jnp.zeros_like(newest)], axis=0)
    slopes[...] = slope_of(newest, spread)
    start = pl.multiple_of(lax.axis_index("elem") * rows, rows)
    slope[...] = slopes[:, pl.ds(start, rows)]


def late_part(late, masked, part, both, longer):
    gusts = late.shape[0] // LATE
    first = lax.axis_index("lag") == 0

    @pl.when(first)
    def _():
        both[...] = part[...]

    @pl.when(jnp.logical_not(first))
    def _():
        longer[...] = jnp.zeros_like(longer)
        longer[: late.shape[0], :] = late[...].astype(jnp.float32)
        acc = part[...]
        for lag in range(LATE):
            lhs = longer[lag * gusts : lag * gusts + part.shape[0], :].astype(jnp.bfloat16)
            acc += dot_rows(lhs, masked[lag])
        both[...] = acc


def known_base(part, forcing, slope, ahead):
    gusts = forcing.shape[1]
    values = []
    for step in range(STEPS):
        at = (STEPS - 1 - step) * gusts
        value = forcing[step] - part[at : at + gusts, :]
        if step == 0:
            value = value + slope[:gusts, :]
        values.append(value)
    values.append(jnp.zeros_like(values[0]))
    ahead[...] = jnp.concatenate(values, axis=0)


def make_base(after, ahead, other, base):
    del after
    gusts = 4
    values = [other[at * gusts : (at + 1) * gusts, :] for at in reversed(range(STEPS))]
    values.append(jnp.zeros_like(values[0]))
    base[...] = ahead[...] - jnp.concatenate(values, axis=0)


def march(
    masked, load_1, load_2, load_3, swap_1, swap_2, swap_3, own_c,
    base_0, base_1, base_2, base_3, spread, out, near_out,
):
    place = lax.axis_index("elem")
    second = lax.axis_index("gust") == 1
    _, rows, total = masked.shape
    cut = rows // 2
    flips_of = range(total // rows)
    loads = (None, load_1, load_2, load_3)
    swaps = (None, swap_1, swap_2, swap_3)

    def flipped(values):
        odd = place % 2 == 1
        high = place // 2 == 1
        near = [jnp.where(odd, values[i ^ 1], values[i]) for i in flips_of]
        return [jnp.where(high, near[i ^ 2], near[i]) for i in flips_of]

    def rows_right(value):
        return jnp.where(second, pltpu.roll(value, cut, 1), value)

    def received(flip, start, count):
        columns = pl.ds(start, count)
        return jnp.concatenate([loads[flip][:, columns], swaps[flip][:, columns]], axis=0)

    def times(fresh_b, lag, flip):
        if flip == 0:
            return dot_rows(fresh_b, masked[lag])
        at = lag * total + (2 * rows if lag == LATE - 1 else 0)
        return rows_right(dot_rows(fresh_b, received(flip, at, total)))

    def corrected(drive, flip):
        lhs = jnp.concatenate(words_of(drive, 2), axis=0)
        added = 0.0
        for word in range(2):
            if flip == 0:
                rhs = own_c[:, word * rows : (word + 1) * rows]
            else:
                rhs = received(flip, (LATE - 1) * total + word * rows, rows)
            both = dot_rows(lhs, rhs)
            added = added + (both[:GUST_ROWS] + both[GUST_ROWS:])
        return drive + (added if flip == 0 else rows_right(added))

    marching = ((place == 1) | (place == 2)) & (lax.axis_index("lag") == 0)

    @pl.when(jnp.logical_not(marching))
    def _():
        out[...] = jnp.zeros_like(out)
        near_out[...] = jnp.zeros_like(near_out)

    @pl.when(marching)
    def _():
        waiting = [
            [base[step * 4 : step * 4 + GUST_ROWS, :] for base in (base_0, base_1, base_2, base_3)]
            for step in range(STEPS)
        ]
        waiting[LATE] = waiting[LATE][:2]
        for step in range(LATE):
            fresh = [corrected(waiting[step][flip], flip) for flip in flips_of]
            out[step], near_out[step] = fresh[:2]
            whole = jnp.concatenate(flipped(fresh), axis=1)
            fresh_b = whole.astype(jnp.bfloat16)
            slope = slope_of(whole, spread)
            slope = flipped([slope[:, i * rows : (i + 1) * rows] for i in flips_of])
            for later in range(step + 1, STEPS):
                lag = later - step - 1
                for flip in range(len(waiting[later])):
                    change = times(fresh_b, lag, flip)
                    if lag == 0:
                        change = change - slope[flip]
                    waiting[later][flip] = waiting[later][flip] - change
        out[LATE], near_out[LATE] = (corrected(waiting[LATE][flip], flip) for flip in (0, 1))


def on_core(body, shapes, operands, scratch=(), in_specs=None, limit=24, name=None, force=False):
    vmem = pl.BlockSpec(memory_space=pltpu.VMEM)
    return pl.pallas_call(
        body,
        out_shape=[
            pltpu.VMEM(shape, dtype) if force else jax.ShapeDtypeStruct(shape, dtype)
            for shape, dtype in shapes
        ],
        in_specs=in_specs or [vmem] * len(operands),
        out_specs=[vmem] * len(shapes),
        scratch_shapes=list(scratch),
        cost_estimate=pl.CostEstimate(flops=10**10, bytes_accessed=2**20, transcendentals=0),
        compiler_params=pltpu.CompilerParams(vmem_limit_bytes=limit * 2**20 if limit else None),
        name=name,
    )(*operands)


def exchanged(value, pairs, count):
    named = {source for source, _ in pairs}
    moves = [(2 * a + core, 2 * b + core) for a, b in pairs for core in (0, 1)]
    moves += [
        (2 * i + core, 2 * i + 1 - core) for i in range(count) if i not in named for core in (0, 1)
    ]
    return lax.ppermute(value, ("elem", "lag", "gust"), moves)


def places_march(history, forcing, interaction, block_mask, correction, neighbours, edge_coef):
    f32, bf16 = jnp.float32, jnp.bfloat16
    rows = correction.shape[0]
    lags, gusts, _ = history.shape
    count = lax.axis_size("elem")
    total = rows * count
    part_rows = 24
    width = (LATE - 1) * total + 2 * rows
    anywhere = pl.BlockSpec(memory_space=pl.ANY)
    vmem = pl.BlockSpec(memory_space=pltpu.VMEM)

    def like(value):
        return pltpu.VMEM(value.shape, value.dtype)

    def crossed(value, axis):
        return lax.ppermute(value, axis, [(0, 1), (1, 0)])

    (message,) = on_core(
        pack,
        [((64, rows), bf16)],
        (history, neighbours, edge_coef),
        scratch=[like(history), like(neighbours), like(edge_coef), pltpu.SemaphoreType.DMA((3,))],
        in_specs=[anywhere] * 3,
        limit=None,
        force=True,
        name="pack",
    )
    messages = flips(message)
    mask = jnp.transpose(block_mask, (1, 2, 0))
    after_message, _ = lax.optimization_barrier((correction, message))
    own_c, near_load = on_core(
        make_near_load,
        [((rows, 2 * rows), bf16), ((rows // 2, width + total), bf16)],
        (mask, interaction, after_message),
        scratch=[
            pltpu.SMEM(mask.shape, mask.dtype),
            pltpu.VMEM((LATE, rows, total), bf16),
            like(correction),
            pltpu.SemaphoreType.DMA((3,)),
        ],
        in_specs=[anywhere] * 3,
        name="near_load",
    )
    masked, mid_load = on_core(
        make_masked,
        [(interaction.shape, bf16), ((rows // 2, width), bf16)],
        (mask, interaction, near_load),
        scratch=[pltpu.SMEM(mask.shape, mask.dtype), pltpu.SemaphoreType.DMA((1,))],
        in_specs=[anywhere, vmem, vmem],
        name="masked",
    )
    everyone, late = on_core(
        order,
        [((64, total), bf16), ((LATE * gusts, total), bf16)],
        [messages[flip] for flip in (0, 2, 3, 1)],
        name="order",
    )
    before = crossed(late, "lag")
    part, slope = on_core(
        main_part,
        [((part_rows, rows), f32), ((GUST_ROWS, rows), f32)],
        (everyone, masked),
        scratch=[
            pltpu.VMEM((56, total), f32),
            pltpu.VMEM((2 * RIM, total), f32),
            pltpu.VMEM((GUST_ROWS, total), f32),
        ],
        name="main_part",
    )

    mid_load, _ = lax.optimization_barrier((mid_load, own_c))

    def bulk(value, pairs):
        return exchanged(value, [(2 * a, 2 * b) for a, b in pairs], 2 * count)

    near = bulk(near_load, NEAR)
    mid = bulk(mid_load, MID)

    (part,) = on_core(
        late_part,
        [((part_rows, rows), f32)],
        (before, masked, part),
        scratch=[pltpu.VMEM((40, total), f32)],
        name="late_part",
    )
    other = crossed(part, "lag")
    (ahead,) = on_core(
        known_base,
        [((part_rows, rows), f32)],
        (part, forcing, slope),
        name="known_base",
    )
    (far_load,) = on_core(
        relay, [((rows // 2, width), bf16)], (ahead, near), in_specs=[anywhere, vmem], name="relay"
    )
    far = bulk(far_load, MID)
    early, _ = lax.optimization_barrier(((near, mid), ahead))
    near_swap, mid_swap = (crossed(piece, "gust") for piece in early)
    (base,) = on_core(
        make_base,
        [((part_rows, rows), f32)],
        (far_load, ahead, other),
        in_specs=[anywhere, vmem, vmem],
        name="base",
    )
    bases = [base] + [bulk(base, pairs) for pairs in (NEAR, FAR, MID)]
    (spread,) = on_core(
        all_spread,
        [((2 * RIM, total), f32)],
        (base, everyone),
        in_specs=[anywhere, vmem],
        name="spread",
    )
    far, _ = lax.optimization_barrier((far, bases[3]))
    far_swap = crossed(far, "gust")
    own, outer = on_core(
        march,
        [((STEPS, GUST_ROWS, rows), f32)] * 2,
        (masked, near, far, mid, near_swap, far_swap, mid_swap, own_c, *bases, spread),
        name="march",
    )

    def handed(value, *cycles):
        moves = []
        for cycle in cycles:
            moves += zip(cycle, cycle[1:] + cycle[:1])
        return exchanged(value, moves, 2 * count)

    to_both = handed(outer, [2, 1, 3], [4, 7, 5])
    to_outer = handed(outer, [2, 0], [4, 6])
    to_lag = handed(own, [2, 3], [4, 5])
    place = lax.axis_index("elem")
    inside = (place == 1) | (place == 2)
    first = lax.axis_index("lag") == 0
    result = jnp.where(
        inside, jnp.where(first, own, to_lag), jnp.where(first, to_outer, to_both)
    )
    return result[:, :gusts]


def solution(mesh):
    placed = (
        P("lag", ("groups", "gust"), "elem"),
        P(None, ("groups", "gust"), "elem"),
        P("lag", "elem", None),
        P("lag", "elem", None),
        P("elem", None),
        P(None, "elem"),
        P(None, "elem"),
    )
    small = mesh.shape["elem"] == 4 and mesh.shape["lag"] == 2 and mesh.shape["gust"] == 2
    return jax.shard_map(
        places_march if small else exchange_each_step,
        mesh=mesh,
        in_specs=placed,
        out_specs=P(None, ("groups", "gust"), "elem"),
        check_vma=False,
    )
```
